256 devices in a mesh: ctx: 64 (over y, x, z_hi, core), head: 4 (over z_lo).
Axes of the slice: x: 4, y: 4, z: 8 (z_hi: 2, z_lo: 4; z = z_hi * 4 + z_lo), core: 2. Of those that a mesh axis runs over, the one named last changes fastest.
Arguments:
- streams: bfloat16 [3, 8192, 4096], P(None, 'ctx', 'head'), may hold values from -6 to 6
- short_taps: float32 [3, 7, 4096], P(None, None, 'head'), may hold values from -2 to 2
- long_taps: float32 [256, 128], P('head'), may hold values from -0.5 to 0.5
- skip_gain: float32 [4096], P('head'), may hold values from -4 to 4
- norm_gain: float32 [4096], replicated, may hold values from 0.5 to 8
- w_qkv: bfloat16 [4096, 3, 2048], P('ctx', None, 'head'), may hold values from -0.09375 to 0.09375
Outputs:
- attended: bfloat16 [8192, 2048], P('ctx', 'head')
The draws below stay inside these ranges and needn't reach their ends.
All inputs are finite; a program needn't handle non-finite values.
Results may differ from the reference program's by a relative error of at most 0.035.
The reference program's roundings to bfloat16 on the way count: a program that leaves them out, or rounds other values in their place, can miss the bound.
Values may be sent and summed in bfloat16 or wider, within the bound.
A program may use at most 128 MiB of HBM per device.

```python
import math
import jax
import jax.numpy as jnp
from jax import lax

D = 4096
HD = 128
AH = 16
FG = 256
SHORT = 7
LONG = 128
TOKENS = 8192


def draw_norm_gain(key, part):
    key = jax.random.fold_in(key, 11)
    return jax.random.uniform(key, (D,), jnp.float32, 0.5, 1.5)


def steps_of(own_key, extent, split, smallest, largest):
    level = 1.0
    for axis_at, parts in split:
        steps = jax.random.uniform(jax.random.fold_in(jax.random.fold_in(own_key, 6), axis_at), (parts,), jnp.float32, smallest / len(split), largest / len(split))
        level = level * jnp.repeat(jnp.exp(steps), extent[axis_at] // parts).reshape((-1,) + (1,) * (len(extent) - 1 - axis_at))
    return level


def scatter_about(rng, dims, deviation, limit, pieces=(), kind=jnp.bfloat16):
    loudness = steps_of(rng, dims, pieces, -0.22, 0.18) if pieces else 1.0
    values = jax.random.normal(rng, dims, jnp.float32) * deviation * loudness
    return jnp.minimum(jnp.maximum(values, -limit), limit).astype(kind)


def setup_inputs(seed: int = 0) -> dict:
    key_list = jax.random.split(jax.random.key(seed), 7)
    streams = scatter_about(key_list[0], (3, TOKENS, D), 1.0, 6.0, ((1, 64), (2, 4)))
    short_taps = scatter_about(key_list[1], (3, SHORT, D), SHORT ** -0.5, 2.0, ((2, 4),), jnp.float32)
    long_taps = scatter_about(key_list[2], (FG, LONG), LONG ** -0.5, 0.5, ((0, 4),), jnp.float32)
    skip_gain = scatter_about(key_list[3], (D,), 1.0, 4.0, ((0, 4),), jnp.float32)
    norm_gain = draw_norm_gain(jax.random.fold_in(key_list[6], 71), 0)
    w_qkv = scatter_about(key_list[5], (D, 3, AH * HD), D ** -0.5, 0.09375, ((0, 64), (2, 4)))
    return dict(streams=streams, short_taps=short_taps, long_taps=long_taps, skip_gain=skip_gain, norm_gain=norm_gain, w_qkv=w_qkv)


def featurize(streams, short_taps):
    values = streams.astype(jnp.float32)
    padded = jnp.pad(values, ((0, 0), (SHORT - 1, 0), (0, 0)))
    result = jnp.zeros(values.shape, jnp.float32)
    for offset in range(SHORT):
        begin = SHORT - 1 - offset
        result = result + short_taps[:, offset][:, None, :] * padded[:, begin:begin + TOKENS]
    return result

def long_filter(gated, long_taps):
    per_channel = jnp.repeat(long_taps, D // FG, axis=0)
    padded = jnp.pad(gated, ((LONG - 1, 0), (0, 0)))

    def add_tap(offset, total):
        tap_index = offset.astype(jnp.int32)
        begin = (LONG - 1 - tap_index).astype(jnp.int32)
        window = lax.dynamic_slice_in_dim(padded, begin, TOKENS, 0)
        column = lax.dynamic_slice_in_dim(per_channel, tap_index, 1, 1)[:, 0]
        return total + column[None, :] * window
    return lax.fori_loop(0, LONG, add_tap, jnp.zeros(gated.shape, jnp.float32))

def attend(query, keys, values):
    scale = 1.0 / math.sqrt(HD)
    block = min(512, TOKENS)
    key_pos = jnp.arange(TOKENS, dtype=jnp.int32)
    keys_wide = keys.astype(jnp.float32)
    values_wide = values.astype(jnp.float32)

    def one_block(index):
        begin = (index * block).astype(jnp.int32)
        rows = lax.dynamic_slice_in_dim(query, begin, block, 0).astype(jnp.float32)
        scores = jnp.einsum('qhd,khd->hqk', rows, keys_wide) * scale
        query_pos = begin + jnp.arange(block, dtype=jnp.int32)
        visible = key_pos[None, None, :] <= query_pos[None, :, None]
        top = lax.optimization_barrier(jnp.max(jnp.where(visible, scores, -jnp.inf), axis=-1, keepdims=True))
        weights = jnp.where(visible, jnp.exp(scores - top), 0.0)
        total = lax.optimization_barrier(jnp.sum(weights, axis=-1))
        rounded = lax.optimization_barrier(weights.astype(jnp.bfloat16)).astype(jnp.float32)
        summed = jnp.einsum('hqk,khd->qhd', rounded, values_wide)
        mixed = summed / jnp.transpose(total)[:, :, None]
        return mixed.reshape(block, AH * HD).astype(jnp.bfloat16)
    blocks = lax.map(one_block, jnp.arange(TOKENS // block, dtype=jnp.int32))
    return blocks.reshape(TOKENS, AH * HD)

def reference(streams, short_taps, long_taps, skip_gain, norm_gain, w_qkv):
    featured = featurize(streams, short_taps)
    gated = featured[1] * featured[2]
    conv = long_filter(gated, long_taps)
    mixed = (featured[0] * (conv + skip_gain[None, :] * gated)).astype(jnp.bfloat16)
    wide = mixed.astype(jnp.float32)
    power = lax.optimization_barrier(jnp.mean(wide * wide, axis=-1, keepdims=True))
    normed = (wide * lax.rsqrt(power + 1e-06) * norm_gain[None, :]).astype(jnp.bfloat16)
    proj = jnp.dot(normed, w_qkv.reshape(D, 3 * AH * HD), preferred_element_type=jnp.float32)
    proj = proj.astype(jnp.bfloat16).reshape(TOKENS, 3, AH, HD)
    return attend(proj[:, 0], proj[:, 1], proj[:, 2])
```

```python
import math

import jax
import jax.numpy as jnp
from jax import lax
from jax.experimental import pallas as pl
from jax.experimental.pallas import tpu as pltpu
from jax.sharding import PartitionSpec as P

HD = 128
TOK = 128
HALF = TOK // 2
UNIT = HALF // 2
CH = 1024
SUP = 512
SHORT = 7
GROUP = 16
MESH = pl.DeviceIdType.MESH
BF = jnp.bfloat16
F32 = jnp.float32


def kernel(
    x_ref, st_ref, taps_ref, skip_ref, gain_ref, w_ref, out_ref,
    rim, ext, ghl, gf, x1f, base, thi, tlo, mall, wsrc, wbuf, kv, qt, acc, lsum, mrow, psum, pacc, att, oland,
    s_halo, r_halo, s_w0, r_w0, s_w, r_w, s_kv, r_kv, s_zp, r_zp, s_zm, r_zm, s_oc, r_oc, s_out, r_out,
):
    c = lax.axis_index("ctx")
    zl = lax.axis_index("head")
    s = c // 4
    r = c % 4
    y, x = s // 4, s % 4
    zh, core = r // 2, r % 2
    z = zh * 4 + zl

    def dev(yy, xx, zz, cc):
        return (((yy * 4 + xx) * 2 + zz // 4) * 2 + cc, zz % 4)

    x_next, x_prev = dev(y, (x + 1) % 4, z, core), dev(y, (x + 3) % 4, z, core)
    y_next, y_prev = dev((y + 1) % 4, x, z, core), dev((y + 3) % 4, x, z, core)
    z_next, z_prev = dev(y, x, (z + 1) % 8, core), dev(y, x, (z + 7) % 8, core)
    other = dev(y, x, z, 1 - core)
    x_far, y_far = dev(y, (x + 2) % 4, z, core), dev((y + 2) % 4, x, z, core)
    mate_at = [(zh, 1 - core), (1 - zh, core), (1 - zh, 1 - core)]
    mate_rank = [a * 2 + b for a, b in mate_at]
    mates = [(s * 4 + rank, zl) for rank in mate_rank]
    c_next, c_prev = ((c + 1) % 64, zl), ((c + 63) % 64, zl)

    pending = []

    def send(src, dst, s_sem, r_sem, to):
        copy = pltpu.make_async_remote_copy(
            src_ref=src, dst_ref=dst, send_sem=s_sem, recv_sem=r_sem, device_id=to, device_id_type=MESH
        )
        copy.start()
        pending.append(copy)

    def recv(dst, s_sem, r_sem, frm):
        pltpu.make_async_remote_copy(
            src_ref=dst, dst_ref=dst, send_sem=s_sem, recv_sem=r_sem, device_id=frm, device_id_type=MESH
        ).wait_recv()

    barrier = pltpu.get_barrier_semaphore()
    partners = [x_next, x_prev, y_next, y_prev, z_next, z_prev, c_next, c_prev, x_far, y_far] + mates
    for p in partners:
        pl.semaphore_signal(barrier, inc=1, device_id=p, device_id_type=MESH)

    for rr in range(4):
        for k in range(3):
            wsrc[rr, :, k * HD : (k + 1) * HD] = w_ref[k, :, rr * HD : (rr + 1) * HD]

    def own_slot(h):
        return (1 - h) * (y * 4 + x) + h * (x * 4 + y)

    pl.semaphore_wait(barrier, len(partners))
    send(x_ref.at[:, pl.ds(TOK - 16, 16), :], rim, s_halo.at[3], r_halo.at[3], c_next)
    mine = wbuf.at[zh, core, own_slot(core)]
    for k in range(3):
        send(wsrc.at[mate_rank[k]], mine, s_w0.at[k], r_w0.at[k], mates[k])
    wbuf[zh, core, own_slot(core)] = wsrc[r]

    def weights_from(k):
        zz, cc = mate_at[k]
        recv(wbuf.at[zz, cc, own_slot(cc)], s_w0.at[k], r_w0.at[k], mates[k])

    def fill(stream, _):
        ext[stream, 16:, :] = x_ref[stream].astype(F32)
        return 0

    lax.fori_loop(0, 3, fill, 0)

    def featured(stream, lo, hi, lanes):
        total = None
        for j in range(SHORT):
            term = st_ref[stream, pl.ds(j, 1), lanes] * ext[stream, pl.ds(16 + lo - j, hi - lo), lanes]
            total = term if total is None else total + term
        return total

    def gate_rows(lo, hi):
        def slab(i, _):
            lanes = pl.ds(pl.multiple_of(i * 128, 128), 128)
            gated = featured(1, lo, hi, lanes) * featured(2, lo, hi, lanes)
            gf[lo:hi, lanes] = gated
            high = gated.astype(BF)
            ghl[i, TOK + lo : TOK + hi, :128] = high
            ghl[i, TOK + lo : TOK + hi, 128:] = (gated - high.astype(F32)).astype(BF)
            return 0
        lax.fori_loop(0, CH // 128, slab, 0)

    def x1_rows(lo, hi):
        def slab(i, _):
            lanes = pl.ds(pl.multiple_of(i * 128, 128), 128)
            x1f[lo:hi, lanes] = featured(0, lo, hi, lanes)
            return 0
        lax.fori_loop(0, CH // 128, slab, 0)

    def gated_rows(lo, count, block):
        return ghl.at[:, pl.ds(TOK * block + lo, count), pl.ds(0, 128)]

    halo = ((HALF, HALF), (16, HALF - 16), (0, 16))

    def halo_send(k):
        send(gated_rows(*halo[k], 1), gated_rows(*halo[k], 0), s_halo.at[k], r_halo.at[k], c_next)

    def halo_recv(k):
        recv(gated_rows(*halo[k], 0), s_halo.at[k], r_halo.at[k], c_prev)

    gate_rows(HALF, TOK)
    halo_send(0)

    def gather_steps(buf, s_sem, r_sem):
        mid = buf.shape[2] // 2

        def parts(h):
            if h == 0:
                return x, y, x_next, x_prev, y_next, y_prev, x_far
            return y, x, y_next, y_prev, x_next, x_prev, y_far

        def slot(a, b):
            return (b % 4) * 4 + a % 4

        def whole(h, a, b):
            return buf.at[h, slot(a, b)]

        def piece(h, a, b, p):
            return buf.at[h, slot(a, b), pl.ds(p * mid, mid), :]

        def go(h, ref, idx, to):
            send(ref, ref, s_sem.at[h, idx], r_sem.at[h, idx], to)

        def come(h, ref, idx, frm):
            recv(ref, s_sem.at[h, idx], r_sem.at[h, idx], frm)

        off = (0, -1, 1, 2)

        def spread(h, i):
            a, b, fn, fp, gn, gp, ff = parts(h)
            ref = whole(h, a + off[i] + 4, b)
            go(h, ref, 4 + i, gn)
            go(h, ref, 8 + i, gp)

        def start():
            for h in (0, 1):
                a, b, fn, fp, gn, gp, ff = parts(h)
                go(h, whole(h, a, b), 0, fn)
                go(h, whole(h, a, b), 1, fp)
                go(h, whole(h, a, b), 2, ff)
            for h in (0, 1):
                spread(h, 0)

        def near():
            for h in (0, 1):
                a, b, fn, fp, gn, gp, ff = parts(h)
                come(h, whole(h, a + 3, b), 0, fp)
                come(h, whole(h, a + 1, b), 1, fn)
            for h in (0, 1):
                spread(h, 1)
                spread(h, 2)

        def far():
            for h in (0, 1):
                a, b, fn, fp, gn, gp, ff = parts(h)
                come(h, whole(h, a + 2, b), 2, ff)
                spread(h, 3)

        def across(i):
            for h in (0, 1):
                a, b, fn, fp, gn, gp, ff = parts(h)
                aa = a + off[i] + 4
                come(h, whole(h, aa, b + 3), 4 + i, gp)
                go(h, piece(h, aa, b + 3, 0), 12 + i, gn)
                come(h, whole(h, aa, b + 1), 8 + i, gn)
                go(h, piece(h, aa, b + 1, 1), 16 + i, gp)

        def last(i):
            for h in (0, 1):
                a, b, fn, fp, gn, gp, ff = parts(h)
                aa = a + off[i] + 4
                come(h, piece(h, aa, b + 2, 0), 12 + i, gp)
                come(h, piece(h, aa, b + 2, 1), 16 + i, gn)

        return start, near, far, across, last

    a_start, a_near, a_far, a_across, a_last = gather_steps(wbuf.at[zh], s_w.at[0], r_w.at[0])
    b_start, b_near, b_far, b_across, b_last = gather_steps(wbuf.at[1 - zh], s_w.at[1], r_w.at[1])

    weights_from(0)
    a_start()
    gate_rows(16, HALF)
    halo_send(1)
    x1_rows(16, TOK)

    def clear(i, _):
        ghl[i, :TOK, 128:] = jnp.zeros((TOK, 128), BF)
        ghl[i, 2 * TOK :, :] = jnp.zeros((HALF, 256), BF)
        return 0

    lax.fori_loop(0, CH // 128, clear, 0)

    turn = lax.broadcasted_iota(jnp.int32, (128, 256), 0) + lax.broadcasted_iota(jnp.int32, (128, 256), 1)
    turn = jnp.where(turn == 128, 1.0, 0.0).astype(BF)
    taps = taps_ref[...]
    taps_high = taps.astype(BF)
    taps_low = (taps - taps_high.astype(F32)).astype(BF)
    base[...] = jnp.dot(taps_high, turn, preferred_element_type=F32) + jnp.dot(
        taps_low, turn, preferred_element_type=F32
    )

    def build(g, _):
        row = jnp.broadcast_to(base[pl.ds(g, 1), :], (HALF, 256))
        rows = pl.ds(pl.multiple_of(g * HALF, HALF), HALF)
        rolled = pltpu.roll(row, 0, 1, stride=1, stride_axis=0)
        high = rolled.astype(BF)
        thi[rows, :] = high
        tlo[rows, :] = (rolled - high.astype(F32)).astype(BF)
        return 0

    lax.fori_loop(0, CH // GROUP, build, 0)

    lane_group = lax.broadcasted_iota(jnp.int32, (HALF, 128), 1) // GROUP
    per = 128 // GROUP

    def convolve(half):
        for k in (0,) if half == 0 else (1, 2):
            halo_recv(k)
        lo = HALF * (1 - half)

        @pl.when(first)
        def _():
            ghl[:, lo : lo + HALF, :128] = jnp.zeros((CH // 128, HALF, 128), BF)

        window = slice(lo, lo + 256)

        def slab(i, _):
            rows = pl.ds(pl.multiple_of(i * per * HALF, per * HALF), per * HALF)
            both = jnp.dot(thi[rows, :], ghl[i, window, :], preferred_element_type=F32)
            rest = jnp.dot(tlo[rows, :], ghl[i, window, :128], preferred_element_type=F32)
            both = both[:, :128] + both[:, 128:] + rest
            conv = both[:HALF]
            for g in range(1, per):
                conv = jnp.where(lane_group == g, both[g * HALF : (g + 1) * HALF], conv)
            lanes = pl.ds(pl.multiple_of(i * 128, 128), 128)
            mixed = x1f[lo : lo + HALF, lanes] * (conv + skip_ref[:, lanes] * gf[lo : lo + HALF, lanes])
            mall[half, zl, pl.ds(pl.multiple_of(r * HALF, HALF), HALF), lanes] = mixed.astype(BF)
            return 0

        lax.fori_loop(0, CH // 128, slab, 0)

    def origin(half, zz, cc, u):
        zz = zz % 8
        return mall.at[half, zz % 4, pl.ds(((zz // 4) * 2 + cc) * HALF + u * UNIT, UNIT), :]

    def square(half, zz, cc, u):
        zz = zz % 8
        at = pl.ds(pl.multiple_of(((zz // 4) * 2 + cc) * HALF + u * UNIT, UNIT), UNIT)
        m = mall[half, zz % 4, at, :].astype(F32)
        m = m * m
        total = m[:, :128]
        for i in range(1, CH // 128):
            total = total + m[:, i * 128 : (i + 1) * 128]
        psum[at, :] += total

    def ring_own(half):
        for u in (0, 1):
            own = origin(half, z, core, u)
            send(own, own, s_zp.at[half, 0, u], r_zp.at[half, 0, u], z_next)
            send(own, own, s_zm.at[half, 0, u], r_zm.at[half, 0, u], z_prev)
        for u in (0, 1):
            own = origin(half, z, core, u)
            send(own, own, s_oc.at[half, 0, u], r_oc.at[half, 0, u], other)

    def ring_step(half, k):
        for u in (0, 1):
            if k < 3 or u == 0:
                ref = origin(half, z + 7 - k, core, u)
                recv(ref, s_zp.at[half, k, u], r_zp.at[half, k, u], z_prev)
                if k + 1 < 3 or (k + 1 == 3 and u == 0):
                    send(ref, ref, s_zp.at[half, k + 1, u], r_zp.at[half, k + 1, u], z_next)
                send(ref, ref, s_oc.at[half, 1 + k, u], r_oc.at[half, 1 + k, u], other)
            if k < 3 or u == 1:
                ref = origin(half, z + 1 + k, core, u)
                recv(ref, s_zm.at[half, k, u], r_zm.at[half, k, u], z_next)
                if k + 1 < 3 or (k + 1 == 3 and u == 1):
                    send(ref, ref, s_zm.at[half, k + 1, u], r_zm.at[half, k + 1, u], z_prev)
                idx = 5 + k if k < 3 else 4
                send(ref, ref, s_oc.at[half, idx, u], r_oc.at[half, idx, u], other)
        if half == 1 and k < 2:
            return
        for u in (0, 1):
            if k < 3 or u == 0:
                square(half, z + 7 - k, core, u)
            if k < 3 or u == 1:
                square(half, z + 1 + k, core, u)

    def from_other(half, idx, step):
        for u in (0, 1):
            recv(origin(half, z + step, 1 - core, u), s_oc.at[half, idx, u], r_oc.at[half, idx, u], other)
            square(half, z + step, 1 - core, u)

    def project(half, zs):
        inv = lax.rsqrt(jnp.sum(psum[...], axis=-1, keepdims=True) * (1.0 / (4 * CH)) + 1e-06)
        for zz in zs:
            normed = (mall[half, zz].astype(F32) * inv * gain_ref[:, zz * CH : (zz + 1) * CH]).astype(BF)
            pieces = []
            for i in range(4):
                for zhi in (0, 1):
                    pieces += [wbuf[zhi, 0, zz * 4 + i], wbuf[zhi, 1, i * 4 + zz]]
            part = jnp.dot(normed, jnp.concatenate(pieces, axis=0), preferred_element_type=F32)
            if zz == 0:
                pacc[...] = part
            else:
                pacc[...] += part

    def place(half):
        proj = pacc[...].astype(BF).astype(F32)
        qt[:, half * 256 : (half + 1) * 256] = jnp.transpose(proj[:, :HD]).astype(BF)
        values = jnp.transpose(proj[:, 2 * HD :]).astype(BF)
        for h in (0, 1):
            kv[half, h, own_slot(h), :128, :] = proj[h * 128 : (h + 1) * 128, HD : 2 * HD].astype(BF)
            kv[half, h, own_slot(h), 128:, :] = values[:, h * 128 : (h + 1) * 128]

    scale = math.log2(math.e) / math.sqrt(HD)

    def position(index):
        half = lax.shift_right_logical(index, 8)
        return (lax.shift_right_logical(index, 6) & 3) * TOK + (1 - half) * HALF + (index & (HALF - 1))

    def scores_of(half, h, index):
        keys = kv[half, h, index, :128, :]
        return jnp.dot(keys, qt[...], preferred_element_type=F32) * scale

    def weigh(units, probs):
        values = jnp.concatenate([kv[half, h, index, 128:, :] for half, h, index in units], axis=1)
        probs = jnp.concatenate([p.astype(BF) for p in probs], axis=0)
        return jnp.dot(values, probs, preferred_element_type=F32)

    def total_of(probs):
        total = probs[0]
        for p in probs[1:]:
            total = total + p
        return jnp.sum(total, axis=0, keepdims=True)

    def absorb_own():
        units = [(half, h, own_slot(h)) for half in (0, 1) for h in (0, 1)]
        q_pos = position(lax.broadcasted_iota(jnp.int32, (128, SUP), 1))
        scores = []
        for half, h, index in units:
            k_pos = position(lax.broadcasted_iota(jnp.int32, (128, SUP), 0) + (half * 256 + h * 128))
            scores.append(jnp.where(k_pos <= q_pos, scores_of(half, h, index), -1e30))
        top = scores[0]
        for t in scores[1:]:
            top = jnp.maximum(top, t)
        top = jnp.max(top, axis=0, keepdims=True)
        probs = [jnp.exp2(t - top) for t in scores]
        mrow[...] = top
        lsum[...] = total_of(probs)
        acc[...] = weigh(units, probs)

    def absorb(units):
        biases = [jnp.where(block < s, 0.0, -1e30) for _, _, _, block in units]
        units = [unit[:3] for unit in units]
        scores = [scores_of(*unit) for unit in units]
        old = mrow[...]
        top = old
        for t, bias in zip(scores, biases):
            top = jnp.maximum(top, jnp.max(t, axis=0, keepdims=True) + bias)
        probs = [jnp.exp2(t - (top - bias)) for t, bias in zip(scores, biases)]
        alpha = jnp.exp2(old - top)
        mrow[...] = top
        lsum[...] = lsum[...] * alpha + total_of(probs)
        acc[...] = acc[...] * alpha + weigh(units, probs)

    def stored(lo, hi):
        def some(j, _):
            h, jj = j // 4, j % 4
            units = []
            for t in range(4):
                units.append((0, h, jj * 4 + t, (1 - h) * (jj * 4 + t) + h * (t * 4 + jj)))
            lowest = (1 - h) * jj * 4 + h * jj

            @pl.when(lowest < s)
            def _():
                absorb(units)
            return 0
        lax.fori_loop(lo, hi, some, 0)

    def arrived(places):
        units = []
        for h, da, db in places:
            a, b = (x, y) if h == 0 else (y, x)
            aa, bb = (a + da + 4) % 4, (b + db + 4) % 4
            units.append((1, h, bb * 4 + aa, bb * 4 + aa if h == 0 else aa * 4 + bb))
        seen = units[0][3] < s
        for unit in units[1:]:
            seen = seen | (unit[3] < s)

        @pl.when(seen)
        def _():
            absorb(units)

    first = c == 0
    recv(rim, s_halo.at[3], r_halo.at[3], c_prev)
    ext[:, :16, :] = jnp.where(first, 0.0, rim[...].astype(F32))
    gate_rows(0, 16)
    halo_send(2)
    x1_rows(0, 16)
    a_near()
    weights_from(1)
    weights_from(2)
    b_start()
    convolve(0)
    ring_own(0)
    psum[...] = jnp.zeros_like(psum)
    a_far()
    a_across(0)
    square(0, z, core, 0)
    square(0, z, core, 1)
    a_across(1)
    a_across(2)
    ring_step(0, 0)
    b_near()
    b_far()
    b_across(0)
    convolve(1)
    ring_own(1)
    a_across(3)
    ring_step(0, 1)
    from_other(0, 0, 0)
    b_across(1)
    b_across(2)
    ring_step(1, 0)
    ring_step(0, 2)
    from_other(0, 1, 7)
    from_other(0, 5, 1)
    b_across(3)
    ring_step(1, 1)
    from_other(0, 2, 6)
    from_other(0, 6, 2)
    ring_step(0, 3)
    from_other(0, 3, 5)
    from_other(0, 7, 3)
    from_other(0, 4, 4)
    for i in range(4):
        a_last(i)
    for i in range(4):
        b_last(i)
    project(0, (0, 1, 2, 3))
    place(0)
    k0_start, k0_near, k0_far, k0_across, k0_last = gather_steps(kv.at[0], s_kv.at[0], r_kv.at[0])
    k0_start()

    psum[...] = jnp.zeros_like(psum)
    ring_step(1, 2)
    square(1, z, core, 0)
    square(1, z, core, 1)
    for k in (0, 1):
        for u in (0, 1):
            square(1, z + 7 - k, core, u)
            square(1, z + 1 + k, core, u)
    from_other(1, 0, 0)
    from_other(1, 1, 7)
    from_other(1, 5, 1)
    k0_near()
    k0_far()
    k0_across(0)
    from_other(1, 2, 6)
    from_other(1, 6, 2)
    ring_step(1, 3)
    k0_across(1)
    k0_across(2)
    from_other(1, 3, 5)
    from_other(1, 7, 3)
    from_other(1, 4, 4)
    k0_across(3)
    project(1, (0, 1, 2, 3))
    place(1)
    k1_start, k1_near, k1_far, k1_across, k1_last = gather_steps(kv.at[1], s_kv.at[1], r_kv.at[1])
    k1_start()
    absorb_own()
    for i in range(4):
        k0_last(i)
    stored(0, 2)
    k1_near()
    k1_across(0)
    stored(2, 4)
    k1_far()
    stored(4, 6)
    k1_across(1)
    k1_across(2)
    stored(6, 8)
    arrived([(0, -1, 0), (0, 1, 0), (1, -1, 0), (1, 1, 0)])
    k1_across(3)
    arrived([(0, 2, 0), (1, 2, 0)])
    off = (0, -1, 1, 2)
    for i in range(4):
        arrived([(0, off[i], -1), (0, off[i], 1), (1, off[i], -1), (1, off[i], 1)])
    for i in (0, 2):
        k1_last(i)
        k1_last(i + 1)
        arrived([(0, off[i], 2), (0, off[i + 1], 2), (1, off[i], 2), (1, off[i + 1], 2)])

    result = jnp.transpose(acc[...] / lsum[...]).astype(BF)
    for half in (0, 1):
        for rr in range(4):
            lo = half * 256 + rr * HALF
            att[rr, HALF * (1 - half) : HALF * (2 - half), :] = result[lo : lo + HALF]
    for k in range(3):
        send(att.at[mate_rank[k]], oland.at[r], s_out.at[k], r_out.at[k], mates[k])
    oland[r] = att[r]
    for k in range(3):
        recv(oland.at[mate_rank[k]], s_out.at[k], r_out.at[k], mates[k])
    for rr in range(4):
        out_ref[:, rr * HD : (rr + 1) * HD] = oland[rr]
    for copy in pending:
        copy.wait_send()


def per_device(streams, short_taps, long_taps, skip_gain, norm_gain, w_qkv):
    vmem = pl.BlockSpec(memory_space=pltpu.VMEM)
    dma = pltpu.SemaphoreType.DMA
    return pl.pallas_call(
        kernel,
        out_shape=jax.ShapeDtypeStruct((TOK, 4 * HD), BF),
        in_specs=[vmem] * 6,
        out_specs=vmem,
        scratch_shapes=[
            pltpu.VMEM((3, 16, CH), BF),
            pltpu.VMEM((3, 16 + TOK, CH), F32),
            pltpu.VMEM((CH // 128, 2 * TOK + HALF, 256), BF),
            pltpu.VMEM((TOK, CH), F32),
            pltpu.VMEM((TOK, CH), F32),
            pltpu.VMEM((64, 256), F32),
            pltpu.VMEM((CH // GROUP * HALF, 256), BF),
            pltpu.VMEM((CH // GROUP * HALF, 256), BF),
            pltpu.VMEM((2, 4, 256, CH), BF),
            pltpu.VMEM((4, 64, 3 * HD), BF),
            pltpu.VMEM((2, 2, 16, 64, 3 * HD), BF),
            pltpu.VMEM((2, 2, 16, 256, HD), BF),
            pltpu.VMEM((HD, SUP), BF),
            pltpu.VMEM((HD, SUP), F32),
            pltpu.VMEM((1, SUP), F32),
            pltpu.VMEM((1, SUP), F32),
            pltpu.VMEM((256, 128), F32),
            pltpu.VMEM((256, 3 * HD), F32),
            pltpu.VMEM((4, TOK, HD), BF),
            pltpu.VMEM((4, TOK, HD), BF),
            dma((4,)), dma((4,)),
            dma((3,)), dma((3,)),
            dma((2, 2, 20)), dma((2, 2, 20)),
            dma((2, 2, 20)), dma((2, 2, 20)),
            dma((2, 4, 2)), dma((2, 4, 2)),
            dma((2, 4, 2)), dma((2, 4, 2)),
            dma((2, 8, 2)), dma((2, 8, 2)),
            dma((3,)), dma((3,)),
        ],
        compiler_params=pltpu.CompilerParams(
            collective_id=0, has_side_effects=True, vmem_limit_bytes=56 * 1024 * 1024
        ),
    )(
        streams,
        short_taps,
        long_taps,
        skip_gain.reshape(1, CH),
        norm_gain.reshape(1, 4 * CH),
        jnp.transpose(w_qkv, (1, 0, 2)),
    )


def solution(mesh):
    in_specs = (
        P(None, "ctx", "head"),
        P(None, None, "head"),
        P("head", None),
        P("head"),
        P(),
        P("ctx", None, "head"),
    )
    return jax.shard_map(
        per_device, mesh=mesh, in_specs=in_specs, out_specs=P("ctx", "head"), check_vma=False
    )
```

```python
import math

import jax
import jax.numpy as jnp
from jax import lax
from jax.experimental import pallas as pl
from jax.experimental.pallas import tpu as pltpu
from jax.sharding import PartitionSpec as P

HD = 128
TOK = 128
HALF = TOK // 2
UNIT = HALF // 2
CH = 1024
SUP = 512
SHORT = 7
GROUP = 16
MESH = pl.DeviceIdType.MESH
BF = jnp.bfloat16
F32 = jnp.float32


def kernel(
    x_hbm, st_ref, taps_ref, skip_ref, gain_ref, w_hbm, out_ref,
    x_ref, w_ref, rim_src, rim, ext, ghl, gf, x1f, base, thi, tlo, mall, wsrc, wbuf, normed, kv, qt, acc, lsum, mrow, psum, att, oland,
    l_in, s_halo, r_halo, s_w0, r_w0, s_w, r_w, s_kv, r_kv, s_zp, r_zp, s_zm, r_zm, s_oc, r_oc, s_out, r_out,
):
    c = lax.axis_index("ctx")
    zl = lax.axis_index("head")
    s = c // 4
    r = c % 4
    y, x = s // 4, s % 4
    zh, core = r // 2, r % 2
    z = zh * 4 + zl

    def dev(yy, xx, zz, cc):
        return (((yy * 4 + xx) * 2 + zz // 4) * 2 + cc, zz % 4)

    x_next, x_prev = dev(y, (x + 1) % 4, z, core), dev(y, (x + 3) % 4, z, core)
    y_next, y_prev = dev((y + 1) % 4, x, z, core), dev((y + 3) % 4, x, z, core)
    z_next, z_prev = dev(y, x, (z + 1) % 8, core), dev(y, x, (z + 7) % 8, core)
    other = dev(y, x, z, 1 - core)
    x_far, y_far = dev(y, (x + 2) % 4, z, core), dev((y + 2) % 4, x, z, core)
    mate_at = [(zh, 1 - core), (1 - zh, core), (1 - zh, 1 - core)]
    mate_rank = [a * 2 + b for a, b in mate_at]
    mates = [(s * 4 + rank, zl) for rank in mate_rank]
    c_next, c_prev = ((c + 1) % 64, zl), ((c + 63) % 64, zl)

    pending = []

    def send(src, dst, s_sem, r_sem, to):
        copy = pltpu.make_async_remote_copy(
            src_ref=src, dst_ref=dst, send_sem=s_sem, recv_sem=r_sem, device_id=to, device_id_type=MESH
        )
        copy.start()
        pending.append(copy)
        return copy

    def recv(dst, s_sem, r_sem, frm):
        pltpu.make_async_remote_copy(
            src_ref=dst, dst_ref=dst, send_sem=s_sem, recv_sem=r_sem, device_id=frm, device_id_type=MESH
        ).wait_recv()

    x_in = pltpu.make_async_copy(x_hbm, x_ref, l_in.at[0])
    x_in.start()
    w_in = pltpu.make_async_copy(w_hbm, w_ref, l_in.at[1])
    w_in.start()

    barrier = pltpu.get_barrier_semaphore()
    partners = [c_next, c_prev] + mates + [x_far, y_far, x_next, x_prev, y_next, y_prev, z_next, z_prev]
    for p in partners:
        pl.semaphore_signal(barrier, inc=1, device_id=p, device_id_type=MESH)

    def own_slot(h):
        return (1 - h) * (y * 4 + x) + h * (x * 4 + y)

    def fill(stream, _):
        ext[stream, 16:, :] = x_ref[stream].astype(F32)
        return 0

    x_in.wait()
    lax.fori_loop(0, 3, fill, 0)

    def featured(stream, lo, hi, lanes):
        total = None
        for j in range(SHORT):
            term = st_ref[stream, pl.ds(j, 1), lanes] * ext[stream, pl.ds(16 + lo - j, hi - lo), lanes]
            total = term if total is None else total + term
        return total

    def gate_rows(lo, hi):
        def slab(i, _):
            lanes = pl.ds(pl.multiple_of(i * 128, 128), 128)
            gated = featured(1, lo, hi, lanes) * featured(2, lo, hi, lanes)
            gf[lo:hi, lanes] = gated
            high = gated.astype(BF)
            ghl[i, TOK + lo : TOK + hi, :128] = high
            ghl[i, TOK + lo : TOK + hi, 128:] = (gated - high.astype(F32)).astype(BF)
            return 0
        lax.fori_loop(0, CH // 128, slab, 0)

    def x1_rows(lo, hi):
        def slab(i, _):
            lanes = pl.ds(pl.multiple_of(i * 128, 128), 128)
            x1f[lo:hi, lanes] = featured(0, lo, hi, lanes)
            return 0
        lax.fori_loop(0, CH // 128, slab, 0)

    def gated_rows(lo, count, block):
        return ghl.at[:, pl.ds(TOK * block + lo, count), pl.ds(0, 128)]

    halo = ((HALF, HALF), (16, HALF - 16), (0, 16))

    def halo_send(k):
        send(gated_rows(*halo[k], 1), gated_rows(*halo[k], 0), s_halo.at[k], r_halo.at[k], c_next)

    def halo_recv(k):
        recv(gated_rows(*halo[k], 0), s_halo.at[k], r_halo.at[k], c_prev)

    gate_rows(HALF, TOK)
    gate_rows(16, HALF)
    x1_rows(16, TOK)

    rows = jnp.concatenate([ext[i, 16 + TOK - 6 :, :] for i in range(3)], axis=0)
    rim_src[:, :CH] = rows[:16].astype(BF)
    rest = jnp.concatenate([rows[16:, i * 128 : (i + 1) * 128] for i in range(8)], axis=0)
    rim_src[:, CH:] = rest.astype(BF)

    w_in.wait()
    for rr in range(4):
        for k in range(3):
            wsrc[rr, :, k * HD : (k + 1) * HD] = w_ref[k, :, rr * HD : (rr + 1) * HD]
    wbuf[zh, core, own_slot(core)] = wsrc[r]

    pl.semaphore_wait(barrier, len(partners))
    send(rim_src, rim, s_halo.at[3], r_halo.at[3], c_next)
    halo_send(0)
    mine = wbuf.at[zh, core, own_slot(core)]

    def weights_to(k):
        send(wsrc.at[mate_rank[k]], mine, s_w0.at[k], r_w0.at[k], mates[k])

    def weights_from(k):
        zz, cc = mate_at[k]
        recv(wbuf.at[zz, cc, own_slot(cc)], s_w0.at[k], r_w0.at[k], mates[k])

    weights_to(0)
    weights_to(1)
    weights_to(2)

    def clear(i, _):
        ghl[i, :TOK, 128:] = jnp.zeros((TOK, 128), BF)
        ghl[i, 2 * TOK :, :] = jnp.zeros((96, 256), BF)
        return 0

    lax.fori_loop(0, CH // 128, clear, 0)
    halo_send(1)

    def gather_steps(buf, s_sem, r_sem):
        mid = buf.shape[2] // 2

        def parts(h):
            first = (x, y, x_next, x_prev, y_next, y_prev, x_far)
            second = (y, x, y_next, y_prev, x_next, x_prev, y_far)
            if isinstance(h, int):
                return second if h else first
            mixed = []
            for p, q in zip(first, second):
                if isinstance(p, tuple):
                    mixed.append(tuple(i * (1 - h) + j * h for i, j in zip(p, q)))
                else:
                    mixed.append(p * (1 - h) + q * h)
            return mixed

        def slot(a, b):
            return (b % 4) * 4 + a % 4

        def whole(h, a, b):
            return buf.at[h, slot(a, b)]

        def piece(h, a, b, p):
            return buf.at[h, slot(a, b), pl.ds(p * mid, mid), :]

        def go(h, ref, idx, to):
            send(ref, ref, s_sem.at[h, idx], r_sem.at[h, idx], to)

        def come(h, ref, idx, frm):
            recv(ref, s_sem.at[h, idx], r_sem.at[h, idx], frm)

        off = (0, -1, 1, 2)

        def spread(h, i):
            a, b, fn, fp, gn, gp, ff = parts(h)
            ref = whole(h, a + off[i] + 4, b)
            go(h, ref, 4 + i, gn)
            go(h, ref, 8 + i, gp)

        def start(hs):
            for h in hs:
                a, b, fn, fp, gn, gp, ff = parts(h)
                go(h, whole(h, a, b), 0, fn)
                go(h, whole(h, a, b), 1, fp)
                go(h, whole(h, a, b), 2, ff)
            for h in hs:
                spread(h, 0)

        def near():
            for h in (0, 1):
                a, b, fn, fp, gn, gp, ff = parts(h)
                come(h, whole(h, a + 3, b), 0, fp)
                come(h, whole(h, a + 1, b), 1, fn)
            for h in (0, 1):
                spread(h, 1)
                spread(h, 2)

        def far():
            for h in (0, 1):
                a, b, fn, fp, gn, gp, ff = parts(h)
                come(h, whole(h, a + 2, b), 2, ff)
                spread(h, 3)

        def across(i):
            for h in (0, 1):
                a, b, fn, fp, gn, gp, ff = parts(h)
                aa = a + off[i] + 4
                come(h, whole(h, aa, b + 3), 4 + i, gp)
                go(h, piece(h, aa, b + 3, 0), 12 + i, gn)
                come(h, whole(h, aa, b + 1), 8 + i, gn)
                go(h, piece(h, aa, b + 1, 1), 16 + i, gp)

        def last(i):
            for h in (0, 1):
                a, b, fn, fp, gn, gp, ff = parts(h)
                aa = a + off[i] + 4
                come(h, piece(h, aa, b + 2, 0), 12 + i, gp)
                come(h, piece(h, aa, b + 2, 1), 16 + i, gn)

        return start, near, far, across, last

    a_start, a_near, a_far, a_across, a_last = gather_steps(wbuf.at[zh], s_w.at[0], r_w.at[0])
    b_start, b_near, b_far, b_across, b_last = gather_steps(wbuf.at[1 - zh], s_w.at[1], r_w.at[1])

    turn = lax.broadcasted_iota(jnp.int32, (128, 256), 0) + lax.broadcasted_iota(jnp.int32, (128, 256), 1)
    turn = jnp.where(turn == 128, 1.0, 0.0).astype(BF)
    taps = taps_ref[...]
    taps_high = taps.astype(BF)
    taps_low = (taps - taps_high.astype(F32)).astype(BF)
    base[...] = jnp.dot(taps_high, turn, preferred_element_type=F32) + jnp.dot(
        taps_low, turn, preferred_element_type=F32
    )

    def build(g, _):
        row = jnp.broadcast_to(base[pl.ds(g, 1), :], (UNIT, 256))
        rows = pl.ds(pl.multiple_of(g * UNIT, UNIT), UNIT)
        rolled = pltpu.roll(row, 0, 1, stride=1, stride_axis=0)
        high = rolled.astype(BF)
        thi[rows, :] = high
        tlo[rows, :] = (rolled - high.astype(F32)).astype(BF)
        return 0

    lax.fori_loop(0, CH // GROUP, build, 0, unroll=8)

    lane_group = lax.broadcasted_iota(jnp.int32, (UNIT, 128), 1) // GROUP
    per = 128 // GROUP

    unit_at = (HALF, HALF + UNIT, UNIT, 0)

    def convolve(u):
        lo = unit_at[u]
        window = slice(lo, lo + 256)

        def slab(i, _):
            rows = pl.ds(pl.multiple_of(i * per * UNIT, per * UNIT), per * UNIT)
            both = jnp.dot(thi[rows, :], ghl[i, window, :], preferred_element_type=F32)
            rest = jnp.dot(tlo[rows, :], ghl[i, window, :128], preferred_element_type=F32)
            both = both[:, :128] + both[:, 128:] + rest
            conv = both[:UNIT]
            for g in range(1, per):
                conv = jnp.where(lane_group == g, both[g * UNIT : (g + 1) * UNIT], conv)
            lanes = pl.ds(pl.multiple_of(i * 128, 128), 128)
            mixed = x1f[lo : lo + UNIT, lanes] * (conv + skip_ref[:, lanes] * gf[lo : lo + UNIT, lanes])
            mall[zh, zl, pl.ds(pl.multiple_of(core * TOK + lo, UNIT), UNIT), lanes] = mixed.astype(BF)
            return 0

        lax.fori_loop(0, CH // 128, slab, 0, unroll=8)

    def halo_ready(k):
        halo_recv(k)
        lo, count = halo[k]

        @pl.when(first)
        def _():
            ghl[:, lo : lo + count, :128] = jnp.zeros((CH // 128, count, 128), BF)

    def rows_of(zz, cc, lo, count):
        zz = zz % 8
        return mall.at[zz // 4, zz % 4, pl.ds(cc * TOK + lo, count), :]

    def unit(zz, cc, u):
        return rows_of(zz, cc, unit_at[u], UNIT)

    def pair(zz, cc, half):
        return rows_of(zz, cc, HALF * (1 - half), HALF)

    def square(zz, cc, half):
        zz = zz % 8
        at = pl.ds(pl.multiple_of(cc * TOK + HALF * (1 - half), HALF), HALF)
        m = mall[zz // 4, zz % 4, at, :].astype(F32)
        m = m * m
        total = m[:, :128]
        for i in range(1, CH // 128):
            total = total + m[:, i * 128 : (i + 1) * 128]
        psum[zz // 4, at, :] += total

    def hand_over(zz, idx, half):
        ref = pair(zz, core, half)
        send(ref, ref, s_oc.at[idx, half], r_oc.at[idx, half], other)

    def ring_own(u):
        convolve(u)
        own = unit(z, core, u)
        send(own, own, s_zp.at[0, u], r_zp.at[0, u], z_next)
        send(own, own, s_zm.at[0, u], r_zm.at[0, u], z_prev)

    def ring_own_rest(half):
        hand_over(z, 0, half)
        square(z, core, half)

    def ring_step(k, u):
        if k < 3 or u % 2 == 0:
            ref = unit(z + 7 - k, core, u)
            recv(ref, s_zp.at[k, u], r_zp.at[k, u], z_prev)
            if k + 1 < 3 or (k + 1 == 3 and u % 2 == 0):
                send(ref, ref, s_zp.at[k + 1, u], r_zp.at[k + 1, u], z_next)
        if k < 3 or u % 2 == 1:
            ref = unit(z + 1 + k, core, u)
            recv(ref, s_zm.at[k, u], r_zm.at[k, u], z_next)
            if k + 1 < 3 or (k + 1 == 3 and u % 2 == 1):
                send(ref, ref, s_zm.at[k + 1, u], r_zm.at[k + 1, u], z_prev)

    def ring_rest(k, half):
        hand_over(z + 7 - k, 1 + k, half)
        if k < 3:
            hand_over(z + 1 + k, 5 + k, half)
        square(z + 7 - k, core, half)
        if k < 3:
            square(z + 1 + k, core, half)

    def from_other(idx, half):
        step = (0, 7, 6, 5, 4, 1, 2, 3)[idx]
        recv(pair(z + step, 1 - core, half), s_oc.at[idx, half], r_oc.at[idx, half], other)
        square(z + step, 1 - core, half)

    def weights(zz, lanes):
        pieces = []
        for i in range(4):
            for zz_hi in (0, 1):
                pieces += [wbuf[zz_hi, 0, zz * 4 + i, :, lanes], wbuf[zz_hi, 1, i * 4 + zz, :, lanes]]
        return jnp.concatenate(pieces, axis=0)

    def keys_values(zhi):
        inv = lax.rsqrt(jnp.sum(psum[zhi], axis=-1, keepdims=True) * (1.0 / (4 * CH)) + 1e-06)
        proj = None
        for zz in range(4):
            rounded = (mall[zhi, zz].astype(F32) * inv * gain_ref[:, zz * CH : (zz + 1) * CH]).astype(BF)
            normed[zhi, zz] = rounded
            part = jnp.dot(rounded, weights(zz, slice(HD, 3 * HD)), preferred_element_type=F32)
            proj = part if proj is None else proj + part
        proj = proj.astype(BF).astype(F32)
        values = jnp.transpose(proj[:, HD:]).astype(BF)
        at = own_slot(zhi)
        kv[zhi, at, :256, :] = proj[:, :HD].astype(BF)
        kv[zhi, at, 256:384, :] = values[:, :128]
        kv[zhi, at, 384:, :] = values[:, 128:]

    def queries():
        for zhi in (0, 1):
            proj = None
            for zz in range(4):
                part = jnp.dot(normed[zhi, zz], weights(zz, slice(0, HD)), preferred_element_type=F32)
                proj = part if proj is None else proj + part
            qt[:, zhi * 256 : (zhi + 1) * 256] = jnp.transpose(proj.astype(BF).astype(F32)).astype(BF)

    scale = math.log2(math.e) / math.sqrt(HD)

    def scores_of(h, index):
        return jnp.dot(kv[h, index, :256, :], qt[...], preferred_element_type=F32) * scale

    def weigh(units, probs):
        values = jnp.concatenate(
            [kv[h, index, lo : lo + 128, :] for h, index in units for lo in (256, 384)], axis=1
        )
        probs = jnp.concatenate([p.astype(BF) for p in probs], axis=0)
        return jnp.dot(values, probs, preferred_element_type=F32)

    def total_of(probs):
        total = probs[0]
        for p in probs[1:]:
            total = total + p
        return jnp.sum(total, axis=0, keepdims=True)

    def absorb_own():
        units = [(h, own_slot(h)) for h in (0, 1)]
        q_pos = lax.broadcasted_iota(jnp.int32, (256, SUP), 1)
        k_pos = lax.broadcasted_iota(jnp.int32, (256, SUP), 0)
        scores = [jnp.where(k_pos + h * 256 <= q_pos, scores_of(h, index), -1e30) for h, index in units]
        top = scores[0]
        for t in scores[1:]:
            top = jnp.maximum(top, t)
        top = jnp.max(top, axis=0, keepdims=True)
        probs = [jnp.exp2(t - top) for t in scores]
        mrow[...] = top
        lsum[...] = total_of(probs)
        acc[...] = weigh(units, probs)

    def absorb(units):
        biases = [jnp.where(block < s, 0.0, -1e30) for _, _, block in units]
        units = [unit[:2] for unit in units]
        scores = [scores_of(*unit) for unit in units]
        old = mrow[...]
        top = old
        for t, bias in zip(scores, biases):
            top = jnp.maximum(top, jnp.max(t, axis=0, keepdims=True) + bias)
        probs = [jnp.exp2(t - (top - bias)) for t, bias in zip(scores, biases)]
        alpha = jnp.exp2(old - top)
        mrow[...] = top
        lsum[...] = lsum[...] * alpha + total_of(probs)
        acc[...] = acc[...] * alpha + weigh(units, probs)

    def arrived(places):
        units = []
        for h, da, db in places:
            a, b = (x, y) if h == 0 else (y, x)
            aa, bb = (a + da + 4) % 4, (b + db + 4) % 4
            units.append((h, bb * 4 + aa, bb * 4 + aa if h == 0 else aa * 4 + bb))
        seen = units[0][2] < s
        for unit in units[1:]:
            seen = seen | (unit[2] < s)

        @pl.when(seen)
        def _():
            absorb(units)

    weights_from(0)
    a_start((0, 1))
    first = c == 0
    recv(rim, s_halo.at[3], r_halo.at[3], c_prev)
    rest = rim[:, CH:].astype(F32)
    rest = jnp.concatenate([rest[2 * i : 2 * i + 2] for i in range(8)], axis=1)
    rows = jnp.concatenate([rim[:, :CH].astype(F32), rest], axis=0)
    rows = jnp.where(first, 0.0, rows)
    for i in range(3):
        ext[i, 10:16, :] = rows[6 * i : 6 * i + 6]
    gate_rows(0, 16)
    halo_send(2)
    x1_rows(0, 16)
    psum[...] = jnp.zeros_like(psum)
    halo_ready(0)
    ring_own(0)
    ring_own(1)
    halo_ready(1)
    ring_own(2)
    ring_own_rest(0)
    a_across(0)
    a_near()
    a_far()
    weights_from(1)
    weights_from(2)
    b_start((0, 1))
    ring_step(0, 0)
    ring_step(0, 1)
    halo_ready(2)
    ring_own(3)
    ring_step(0, 2)
    ring_own_rest(1)
    ring_rest(0, 0)
    from_other(0, 0)
    a_across(1)
    a_across(2)
    a_across(3)
    ring_step(1, 0)
    ring_step(1, 1)
    ring_step(0, 3)
    ring_rest(1, 0)
    ring_rest(0, 1)
    from_other(1, 0)
    from_other(5, 0)
    ring_step(1, 2)
    b_across(0)
    b_near()
    b_far()
    from_other(0, 1)
    ring_step(2, 0)
    ring_step(2, 1)
    ring_step(1, 3)
    ring_rest(2, 0)
    ring_rest(1, 1)
    for i in range(4):
        a_last(i)
    b_across(1)
    b_across(2)
    b_across(3)
    from_other(2, 0)
    from_other(6, 0)
    from_other(1, 1)
    from_other(5, 1)
    ring_step(2, 2)
    ring_step(3, 0)
    ring_step(3, 1)
    ring_step(2, 3)
    ring_rest(3, 0)
    ring_rest(2, 1)
    from_other(3, 0)
    from_other(7, 0)
    from_other(2, 1)
    from_other(6, 1)
    from_other(4, 0)
    from_other(3, 1)
    from_other(7, 1)
    for i in range(4):
        b_last(i)
    k_start, k_near, k_far, k_across, k_last = gather_steps(kv, s_kv, r_kv)
    keys_values(zh)
    k_start((zh,))
    ring_step(3, 2)
    ring_step(3, 3)
    ring_rest(3, 1)
    from_other(4, 1)
    keys_values(1 - zh)
    k_start((1 - zh,))
    queries()
    absorb_own()
    off = (0, -1, 1, 2)

    def across_arrived(i):
        for h in (0, 1):
            arrived([(h, off[i], -1), (h, off[i], 1)])

    k_across(0)
    k_near()
    k_far()
    across_arrived(0)
    for h in (0, 1):
        arrived([(h, -1, 0), (h, 1, 0)])
    k_across(1)
    k_across(2)
    arrived([(0, 2, 0), (1, 2, 0)])
    across_arrived(1)
    k_across(3)
    across_arrived(2)
    across_arrived(3)
    for i in range(4):
        k_last(i)
        arrived([(0, off[i], 2), (1, off[i], 2)])

    result = jnp.transpose(acc[...] / lsum[...]).astype(BF)
    for rr in range(4):
        att[rr] = result[rr * TOK : (rr + 1) * TOK]
    for k in (1, 2, 0):
        send(att.at[mate_rank[k]], oland.at[r], s_out.at[k], r_out.at[k], mates[k])
    oland[r] = att[r]
    for k in range(3):
        recv(oland.at[mate_rank[k]], s_out.at[k], r_out.at[k], mates[k])
    for rr in range(4):
        out_ref[:, rr * HD : (rr + 1) * HD] = oland[rr]
    for copy in pending:
        copy.wait_send()


def per_device(streams, short_taps, long_taps, skip_gain, norm_gain, w_qkv):
    vmem = pl.BlockSpec(memory_space=pltpu.VMEM)
    dma = pltpu.SemaphoreType.DMA
    return pl.pallas_call(
        kernel,
        out_shape=jax.ShapeDtypeStruct((TOK, 4 * HD), BF),
        in_specs=[pl.BlockSpec(memory_space=pl.ANY)] + [vmem] * 4 + [pl.BlockSpec(memory_space=pl.ANY)],
        out_specs=vmem,
        scratch_shapes=[
            pltpu.VMEM((3, TOK, CH), BF),
            pltpu.VMEM((3, 64, 4 * HD), BF),
            pltpu.VMEM((16, CH + 128), BF),
            pltpu.VMEM((16, CH + 128), BF),
            pltpu.VMEM((3, 16 + TOK, CH), F32),
            pltpu.VMEM((CH // 128, 2 * TOK + 96, 256), BF),
            pltpu.VMEM((TOK, CH), F32),
            pltpu.VMEM((TOK, CH), F32),
            pltpu.VMEM((64, 256), F32),
            pltpu.VMEM((CH // GROUP * UNIT, 256), BF),
            pltpu.VMEM((CH // GROUP * UNIT, 256), BF),
            pltpu.VMEM((2, 4, 256, CH), BF),
            pltpu.VMEM((4, 64, 3 * HD), BF),
            pltpu.VMEM((2, 2, 16, 64, 3 * HD), BF),
            pltpu.VMEM((2, 4, 256, CH), BF),
            pltpu.VMEM((2, 16, 512, HD), BF),
            pltpu.VMEM((HD, SUP), BF),
            pltpu.VMEM((HD, SUP), F32),
            pltpu.VMEM((1, SUP), F32),
            pltpu.VMEM((1, SUP), F32),
            pltpu.VMEM((2, 256, 128), F32),
            pltpu.VMEM((4, TOK, HD), BF),
            pltpu.VMEM((4, TOK, HD), BF),
            dma((2,)),
            dma((4,)), dma((4,)),
            dma((3,)), dma((3,)),
            dma((2, 2, 20)), dma((2, 2, 20)),
            dma((2, 20)), dma((2, 20)),
            dma((4, 4)), dma((4, 4)),
            dma((4, 4)), dma((4, 4)),
            dma((8, 2)), dma((8, 2)),
            dma((3,)), dma((3,)),
        ],
        compiler_params=pltpu.CompilerParams(
            collective_id=0, has_side_effects=True, vmem_limit_bytes=56 * 1024 * 1024
        ),
    )(
        streams,
        short_taps,
        long_taps,
        skip_gain.reshape(1, CH),
        norm_gain.reshape(1, 4 * CH),
        jnp.transpose(w_qkv, (1, 0, 2)),
    )


def solution(mesh):
    in_specs = (
        P(None, "ctx", "head"),
        P(None, None, "head"),
        P("head", None),
        P("head"),
        P(),
        P("ctx", None, "head"),
    )
    return jax.shard_map(
        per_device, mesh=mesh, in_specs=in_specs, out_specs=P("ctx", "head"), check_vma=False
    )
```

```python
import math

import jax
import jax.numpy as jnp
from jax import lax
from jax.experimental import pallas as pl
from jax.experimental.pallas import tpu as pltpu
from jax.sharding import PartitionSpec as P

HD = 128
TOK = 128
HALF = TOK // 2
UNIT = HALF // 2
CH = 1024
SUP = 512
SHORT = 7
GROUP = 16
MESH = pl.DeviceIdType.MESH
BF = jnp.bfloat16
F32 = jnp.float32


def kernel(
    x_hbm, st_ref, taps_ref, skip_ref, gain_ref, w_hbm, out_ref,
    x_ref, w_ref, rim_src, rim, ext, ghl, gf, x1f, base, thi, tlo, mall, wsrc, wbuf, normed, kv, qt, acc, lsum, mrow, psum, att, oland,
    l_in, s_halo, r_halo, s_w0, r_w0, s_w, r_w, s_kv, r_kv, s_zp, r_zp, s_zm, r_zm, s_oc, r_oc, s_out, r_out,
):
    c = lax.axis_index("ctx")
    zl = lax.axis_index("head")
    s = c // 4
    r = c % 4
    y, x = s // 4, s % 4
    zh, core = r // 2, r % 2
    z = zh * 4 + zl

    def dev(yy, xx, zz, cc):
        return (((yy * 4 + xx) * 2 + zz // 4) * 2 + cc, zz % 4)

    x_next, x_prev = dev(y, (x + 1) % 4, z, core), dev(y, (x + 3) % 4, z, core)
    y_next, y_prev = dev((y + 1) % 4, x, z, core), dev((y + 3) % 4, x, z, core)
    z_next, z_prev = dev(y, x, (z + 1) % 8, core), dev(y, x, (z + 7) % 8, core)
    other = dev(y, x, z, 1 - core)
    x_far, y_far = dev(y, (x + 2) % 4, z, core), dev((y + 2) % 4, x, z, core)
    mate_at = [(zh, 1 - core), (1 - zh, core), (1 - zh, 1 - core)]
    mate_rank = [a * 2 + b for a, b in mate_at]
    mates = [(s * 4 + rank, zl) for rank in mate_rank]
    c_next, c_prev = ((c + 1) % 64, zl), ((c + 63) % 64, zl)

    pending = []

    def send(src, dst, s_sem, r_sem, to):
        copy = pltpu.make_async_remote_copy(
            src_ref=src, dst_ref=dst, send_sem=s_sem, recv_sem=r_sem, device_id=to, device_id_type=MESH
        )
        copy.start()
        pending.append(copy)
        return copy

    def recv(dst, s_sem, r_sem, frm):
        pltpu.make_async_remote_copy(
            src_ref=dst, dst_ref=dst, send_sem=s_sem, recv_sem=r_sem, device_id=frm, device_id_type=MESH
        ).wait_recv()

    x_in = pltpu.make_async_copy(x_hbm, x_ref, l_in.at[0])
    x_in.start()
    w_in = pltpu.make_async_copy(w_hbm, w_ref, l_in.at[1])
    w_in.start()

    barrier = pltpu.get_barrier_semaphore()
    partners = [c_next, c_prev] + mates + [x_far, y_far, x_next, x_prev, y_next, y_prev, z_next, z_prev]
    for p in partners:
        pl.semaphore_signal(barrier, inc=1, device_id=p, device_id_type=MESH)

    def own_slot(h):
        return (1 - h) * (y * 4 + x) + h * (x * 4 + y)

    def fill(stream, _):
        ext[stream, 16:, :] = x_ref[stream].astype(F32)
        return 0

    x_in.wait()
    lax.fori_loop(0, 3, fill, 0)

    def featured(stream, lo, hi, lanes):
        total = None
        for j in range(SHORT):
            term = st_ref[stream, pl.ds(j, 1), lanes] * ext[stream, pl.ds(16 + lo - j, hi - lo), lanes]
            total = term if total is None else total + term
        return total

    def gate_rows(lo, hi):
        def slab(i, _):
            lanes = pl.ds(pl.multiple_of(i * 128, 128), 128)
            gated = featured(1, lo, hi, lanes) * featured(2, lo, hi, lanes)
            gf[lo:hi, lanes] = gated
            high = gated.astype(BF)
            ghl[i, TOK + lo : TOK + hi, :128] = high
            ghl[i, TOK + lo : TOK + hi, 128:] = (gated - high.astype(F32)).astype(BF)
            return 0
        lax.fori_loop(0, CH // 128, slab, 0)

    def x1_rows(lo, hi):
        def slab(i, _):
            lanes = pl.ds(pl.multiple_of(i * 128, 128), 128)
            x1f[lo:hi, lanes] = featured(0, lo, hi, lanes)
            return 0
        lax.fori_loop(0, CH // 128, slab, 0)

    def gated_rows(lo, count, block):
        return ghl.at[:, pl.ds(TOK * block + lo, count), pl.ds(0, 128)]

    halo = ((HALF, HALF), (16, HALF - 16), (0, 16))

    def halo_send(k):
        send(gated_rows(*halo[k], 1), gated_rows(*halo[k], 0), s_halo.at[k], r_halo.at[k], c_next)

    def halo_recv(k):
        recv(gated_rows(*halo[k], 0), s_halo.at[k], r_halo.at[k], c_prev)

    gate_rows(HALF, TOK)
    gate_rows(16, HALF)
    x1_rows(16, TOK)

    rows = jnp.concatenate([ext[i, 16 + TOK - 6 :, :] for i in range(3)], axis=0)
    rim_src[:, :CH] = rows[:16].astype(BF)
    rest = jnp.concatenate([rows[16:, i * 128 : (i + 1) * 128] for i in range(8)], axis=0)
    rim_src[:, CH:] = rest.astype(BF)

    w_in.wait()
    for rr in range(4):
        for k in range(3):
            wsrc[rr, :, k * HD : (k + 1) * HD] = w_ref[k, :, rr * HD : (rr + 1) * HD]
    wbuf[zh, core, own_slot(core)] = wsrc[r]

    pl.semaphore_wait(barrier, len(partners))
    send(rim_src, rim, s_halo.at[3], r_halo.at[3], c_next)
    halo_send(0)
    mine = wbuf.at[zh, core, own_slot(core)]

    def weights_to(k):
        send(wsrc.at[mate_rank[k]], mine, s_w0.at[k], r_w0.at[k], mates[k])

    def weights_from(k):
        zz, cc = mate_at[k]
        recv(wbuf.at[zz, cc, own_slot(cc)], s_w0.at[k], r_w0.at[k], mates[k])

    weights_to(0)
    weights_to(1)
    weights_to(2)

    def clear(i, _):
        ghl[i, :TOK, 128:] = jnp.zeros((TOK, 128), BF)
        ghl[i, 2 * TOK :, :] = jnp.zeros((96, 256), BF)
        return 0

    lax.fori_loop(0, CH // 128, clear, 0)
    halo_send(1)

    def gather_steps(buf, s_sem, r_sem, relay=False):
        mid = buf.shape[2] // 2

        def parts(h):
            first = (x, y, x_next, x_prev, y_next, y_prev, x_far)
            second = (y, x, y_next, y_prev, x_next, x_prev, y_far)
            if isinstance(h, int):
                return second if h else first
            mixed = []
            for p, q in zip(first, second):
                if isinstance(p, tuple):
                    mixed.append(tuple(i * (1 - h) + j * h for i, j in zip(p, q)))
                else:
                    mixed.append(p * (1 - h) + q * h)
            return mixed

        def slot(a, b):
            return (b % 4) * 4 + a % 4

        def whole(h, a, b):
            return buf.at[h, slot(a, b)]

        def piece(h, a, b, p):
            return buf.at[h, slot(a, b), pl.ds(p * mid, mid), :]

        def go(h, ref, idx, to):
            send(ref, ref, s_sem.at[h, idx], r_sem.at[h, idx], to)

        def come(h, ref, idx, frm):
            recv(ref, s_sem.at[h, idx], r_sem.at[h, idx], frm)

        off = (0, -1, 1, 2)

        def spread(h, i):
            a, b, fn, fp, gn, gp, ff = parts(h)
            ref = whole(h, a + off[i] + 4, b)
            go(h, ref, 4 + i, gn)
            go(h, ref, 8 + i, gp)

        def start(hs):
            for h in hs:
                a, b, fn, fp, gn, gp, ff = parts(h)
                go(h, whole(h, a, b), 0, fn)
                go(h, whole(h, a, b), 1, fp)
                if not relay:
                    go(h, whole(h, a, b), 2, ff)
            for h in hs:
                spread(h, 0)

        def near():
            for h in (0, 1):
                a, b, fn, fp, gn, gp, ff = parts(h)
                come(h, whole(h, a + 3, b), 0, fp)
                if relay:
                    go(h, piece(h, a + 3, b, 0), 2, fn)
                come(h, whole(h, a + 1, b), 1, fn)
                if relay:
                    go(h, piece(h, a + 1, b, 1), 3, fp)
            for h in (0, 1):
                spread(h, 1)
                spread(h, 2)

        def far():
            for h in (0, 1):
                a, b, fn, fp, gn, gp, ff = parts(h)
                if relay:
                    come(h, piece(h, a + 2, b, 0), 2, fp)
                    come(h, piece(h, a + 2, b, 1), 3, fn)
                else:
                    come(h, whole(h, a + 2, b), 2, ff)
                spread(h, 3)

        def across(i):
            for h in (0, 1):
                a, b, fn, fp, gn, gp, ff = parts(h)
                aa = a + off[i] + 4
                come(h, whole(h, aa, b + 3), 4 + i, gp)
                go(h, piece(h, aa, b + 3, 0), 12 + i, gn)
                come(h, whole(h, aa, b + 1), 8 + i, gn)
                go(h, piece(h, aa, b + 1, 1), 16 + i, gp)

        def last(i):
            for h in (0, 1):
                a, b, fn, fp, gn, gp, ff = parts(h)
                aa = a + off[i] + 4
                come(h, piece(h, aa, b + 2, 0), 12 + i, gp)
                come(h, piece(h, aa, b + 2, 1), 16 + i, gn)

        return start, near, far, across, last

    a_start, a_near, a_far, a_across, a_last = gather_steps(wbuf.at[zh], s_w.at[0], r_w.at[0])
    b_start, b_near, b_far, b_across, b_last = gather_steps(wbuf.at[1 - zh], s_w.at[1], r_w.at[1])

    turn = lax.broadcasted_iota(jnp.int32, (128, 256), 0) + lax.broadcasted_iota(jnp.int32, (128, 256), 1)
    turn = jnp.where(turn == 128, 1.0, 0.0).astype(BF)
    taps = taps_ref[...]
    taps_high = taps.astype(BF)
    taps_low = (taps - taps_high.astype(F32)).astype(BF)
    base[...] = jnp.dot(taps_high, turn, preferred_element_type=F32) + jnp.dot(
        taps_low, turn, preferred_element_type=F32
    )

    def build(g, _):
        row = jnp.broadcast_to(base[pl.ds(g, 1), :], (UNIT, 256))
        rows = pl.ds(pl.multiple_of(g * UNIT, UNIT), UNIT)
        rolled = pltpu.roll(row, 0, 1, stride=1, stride_axis=0)
        high = rolled.astype(BF)
        thi[rows, :] = high
        tlo[rows, :] = (rolled - high.astype(F32)).astype(BF)
        return 0

    lax.fori_loop(0, CH // GROUP, build, 0, unroll=8)

    lane_group = lax.broadcasted_iota(jnp.int32, (UNIT, 128), 1) // GROUP
    per = 128 // GROUP

    unit_at = (HALF, HALF + UNIT, UNIT, 0)

    def convolve(u):
        lo = unit_at[u]
        window = slice(lo, lo + 256)

        def slab(i, _):
            rows = pl.ds(pl.multiple_of(i * per * UNIT, per * UNIT), per * UNIT)
            both = jnp.dot(thi[rows, :], ghl[i, window, :], preferred_element_type=F32)
            rest = jnp.dot(tlo[rows, :], ghl[i, window, :128], preferred_element_type=F32)
            both = both[:, :128] + both[:, 128:] + rest
            conv = both[:UNIT]
            for g in range(1, per):
                conv = jnp.where(lane_group == g, both[g * UNIT : (g + 1) * UNIT], conv)
            lanes = pl.ds(pl.multiple_of(i * 128, 128), 128)
            mixed = x1f[lo : lo + UNIT, lanes] * (conv + skip_ref[:, lanes] * gf[lo : lo + UNIT, lanes])
            mall[zh, zl, pl.ds(pl.multiple_of(core * TOK + lo, UNIT), UNIT), lanes] = mixed.astype(BF)
            return 0

        lax.fori_loop(0, CH // 128, slab, 0, unroll=8)

    def halo_ready(k):
        halo_recv(k)
        lo, count = halo[k]

        @pl.when(first)
        def _():
            ghl[:, lo : lo + count, :128] = jnp.zeros((CH // 128, count, 128), BF)

    def rows_of(zz, cc, lo, count):
        zz = zz % 8
        return mall.at[zz // 4, zz % 4, pl.ds(cc * TOK + lo, count), :]

    def unit(zz, cc, u):
        return rows_of(zz, cc, unit_at[u], UNIT)

    def pair(zz, cc, half):
        return rows_of(zz, cc, HALF * (1 - half), HALF)

    def square(zz, cc, half):
        zz = zz % 8
        at = pl.ds(pl.multiple_of(cc * TOK + HALF * (1 - half), HALF), HALF)
        m = mall[zz // 4, zz % 4, at, :].astype(F32)
        m = m * m
        total = m[:, :128]
        for i in range(1, CH // 128):
            total = total + m[:, i * 128 : (i + 1) * 128]
        psum[zz // 4, at, :] += total

    def hand_over(zz, idx, half):
        ref = pair(zz, core, half)
        send(ref, ref, s_oc.at[idx, half], r_oc.at[idx, half], other)

    def ring_own(u):
        convolve(u)
        own = unit(z, core, u)
        send(own, own, s_zp.at[0, u], r_zp.at[0, u], z_next)
        send(own, own, s_zm.at[0, u], r_zm.at[0, u], z_prev)

    def ring_own_rest(half):
        hand_over(z, 0, half)
        square(z, core, half)

    def ring_step(k, u):
        if k < 3 or u % 2 == 0:
            ref = unit(z + 7 - k, core, u)
            recv(ref, s_zp.at[k, u], r_zp.at[k, u], z_prev)
            if k + 1 < 3 or (k + 1 == 3 and u % 2 == 0):
                send(ref, ref, s_zp.at[k + 1, u], r_zp.at[k + 1, u], z_next)
        if k < 3 or u % 2 == 1:
            ref = unit(z + 1 + k, core, u)
            recv(ref, s_zm.at[k, u], r_zm.at[k, u], z_next)
            if k + 1 < 3 or (k + 1 == 3 and u % 2 == 1):
                send(ref, ref, s_zm.at[k + 1, u], r_zm.at[k + 1, u], z_prev)

    def ring_rest(k, half):
        hand_over(z + 7 - k, 1 + k, half)
        if k < 3:
            hand_over(z + 1 + k, 5 + k, half)
        square(z + 7 - k, core, half)
        if k < 3:
            square(z + 1 + k, core, half)

    def from_other(idx, half):
        step = (0, 7, 6, 5, 4, 1, 2, 3)[idx]
        recv(pair(z + step, 1 - core, half), s_oc.at[idx, half], r_oc.at[idx, half], other)
        square(z + step, 1 - core, half)

    def weights(zz, lanes):
        pieces = []
        for i in range(4):
            for zz_hi in (0, 1):
                pieces += [wbuf[zz_hi, 0, zz * 4 + i, :, lanes], wbuf[zz_hi, 1, i * 4 + zz, :, lanes]]
        return jnp.concatenate(pieces, axis=0)

    def keys_values(zhi):
        inv = lax.rsqrt(jnp.sum(psum[zhi], axis=-1, keepdims=True) * (1.0 / (4 * CH)) + 1e-06)
        proj = None
        for zz in range(4):
            rounded = (mall[zhi, zz].astype(F32) * inv * gain_ref[:, zz * CH : (zz + 1) * CH]).astype(BF)
            normed[zhi, zz] = rounded
            part = jnp.dot(rounded, weights(zz, slice(HD, 3 * HD)), preferred_element_type=F32)
            proj = part if proj is None else proj + part
        proj = proj.astype(BF).astype(F32)
        values = jnp.transpose(proj[:, HD:]).astype(BF)
        at = own_slot(zhi)
        kv[zhi, at, :256, :] = proj[:, :HD].astype(BF)
        kv[zhi, at, 256:384, :] = values[:, :128]
        kv[zhi, at, 384:, :] = values[:, 128:]

    def queries():
        for zhi in (0, 1):
            proj = None
            for zz in range(4):
                part = jnp.dot(normed[zhi, zz], weights(zz, slice(0, HD)), preferred_element_type=F32)
                proj = part if proj is None else proj + part
            qt[:, zhi * 256 : (zhi + 1) * 256] = jnp.transpose(proj.astype(BF).astype(F32)).astype(BF)

    scale = math.log2(math.e) / math.sqrt(HD)

    def scores_of(h, index):
        return jnp.dot(kv[h, index, :256, :], qt[...], preferred_element_type=F32) * scale

    def weigh(units, probs):
        values = jnp.concatenate(
            [kv[h, index, lo : lo + 128, :] for h, index in units for lo in (256, 384)], axis=1
        )
        probs = jnp.concatenate([p.astype(BF) for p in probs], axis=0)
        return jnp.dot(values, probs, preferred_element_type=F32)

    def total_of(probs):
        total = probs[0]
        for p in probs[1:]:
            total = total + p
        return jnp.sum(total, axis=0, keepdims=True)

    def absorb_own():
        units = [(h, own_slot(h)) for h in (0, 1)]
        q_pos = lax.broadcasted_iota(jnp.int32, (256, SUP), 1)
        k_pos = lax.broadcasted_iota(jnp.int32, (256, SUP), 0)
        scores = [jnp.where(k_pos + h * 256 <= q_pos, scores_of(h, index), -1e30) for h, index in units]
        top = scores[0]
        for t in scores[1:]:
            top = jnp.maximum(top, t)
        top = jnp.max(top, axis=0, keepdims=True)
        probs = [jnp.exp2(t - top) for t in scores]
        mrow[...] = top
        lsum[...] = total_of(probs)
        acc[...] = weigh(units, probs)

    def absorb(units):
        biases = [jnp.where(block < s, 0.0, -1e30) for _, _, block in units]
        units = [unit[:2] for unit in units]
        scores = [scores_of(*unit) for unit in units]
        old = mrow[...]
        top = old
        for t, bias in zip(scores, biases):
            top = jnp.maximum(top, jnp.max(t, axis=0, keepdims=True) + bias)
        probs = [jnp.exp2(t - (top - bias)) for t, bias in zip(scores, biases)]
        alpha = jnp.exp2(old - top)
        mrow[...] = top
        lsum[...] = lsum[...] * alpha + total_of(probs)
        acc[...] = acc[...] * alpha + weigh(units, probs)

    def arrived(places):
        units = []
        for h, da, db in places:
            a, b = (x, y) if h == 0 else (y, x)
            aa, bb = (a + da + 4) % 4, (b + db + 4) % 4
            units.append((h, bb * 4 + aa, bb * 4 + aa if h == 0 else aa * 4 + bb))
        seen = units[0][2] < s
        for unit in units[1:]:
            seen = seen | (unit[2] < s)

        @pl.when(seen)
        def _():
            absorb(units)

    weights_from(0)
    a_start((0, 1))
    first = c == 0
    recv(rim, s_halo.at[3], r_halo.at[3], c_prev)
    rest = rim[:, CH:].astype(F32)
    rest = jnp.concatenate([rest[2 * i : 2 * i + 2] for i in range(8)], axis=1)
    rows = jnp.concatenate([rim[:, :CH].astype(F32), rest], axis=0)
    rows = jnp.where(first, 0.0, rows)
    for i in range(3):
        ext[i, 10:16, :] = rows[6 * i : 6 * i + 6]
    gate_rows(0, 16)
    halo_send(2)
    x1_rows(0, 16)
    psum[...] = jnp.zeros_like(psum)
    halo_ready(0)
    ring_own(0)
    ring_own(1)
    halo_ready(1)
    ring_own(2)
    ring_own_rest(0)
    a_across(0)
    a_near()
    a_far()
    weights_from(1)
    weights_from(2)
    b_start((0, 1))
    ring_step(0, 0)
    ring_step(0, 1)
    halo_ready(2)
    ring_own(3)
    ring_step(0, 2)
    ring_own_rest(1)
    ring_rest(0, 0)
    from_other(0, 0)
    a_across(1)
    a_across(2)
    a_across(3)
    ring_step(1, 0)
    ring_step(1, 1)
    ring_step(0, 3)
    ring_rest(1, 0)
    ring_rest(0, 1)
    from_other(1, 0)
    from_other(5, 0)
    ring_step(1, 2)
    b_across(0)
    b_near()
    b_far()
    from_other(0, 1)
    ring_step(2, 0)
    ring_step(2, 1)
    ring_step(1, 3)
    ring_rest(2, 0)
    ring_rest(1, 1)
    for i in range(4):
        a_last(i)
    b_across(1)
    b_across(2)
    b_across(3)
    from_other(2, 0)
    from_other(6, 0)
    from_other(1, 1)
    from_other(5, 1)
    ring_step(2, 2)
    ring_step(3, 0)
    ring_step(3, 1)
    ring_step(2, 3)
    ring_rest(3, 0)
    ring_rest(2, 1)
    from_other(3, 0)
    from_other(7, 0)
    from_other(2, 1)
    from_other(6, 1)
    from_other(4, 0)
    from_other(3, 1)
    from_other(7, 1)
    for i in range(4):
        b_last(i)
    k_start, k_near, k_far, k_across, k_last = gather_steps(kv, s_kv, r_kv, relay=True)
    keys_values(zh)
    k_start((zh,))
    ring_step(3, 2)
    ring_step(3, 3)
    ring_rest(3, 1)
    from_other(4, 1)
    keys_values(1 - zh)
    k_start((1 - zh,))
    queries()
    absorb_own()
    off = (0, -1, 1, 2)

    def across_arrived(i):
        for h in (0, 1):
            arrived([(h, off[i], -1), (h, off[i], 1)])

    k_across(0)
    k_near()
    k_far()
    across_arrived(0)
    for h in (0, 1):
        arrived([(h, -1, 0), (h, 1, 0)])
    k_across(1)
    k_across(2)
    arrived([(0, 2, 0), (1, 2, 0)])
    across_arrived(1)
    k_across(3)
    across_arrived(2)
    across_arrived(3)
    for i in range(4):
        k_last(i)
        arrived([(0, off[i], 2), (1, off[i], 2)])

    result = jnp.transpose(acc[...] / lsum[...]).astype(BF)
    for rr in range(4):
        att[rr] = result[rr * TOK : (rr + 1) * TOK]
    for k in (1, 2, 0):
        send(att.at[mate_rank[k]], oland.at[r], s_out.at[k], r_out.at[k], mates[k])
    oland[r] = att[r]
    for k in range(3):
        recv(oland.at[mate_rank[k]], s_out.at[k], r_out.at[k], mates[k])
    for rr in range(4):
        out_ref[:, rr * HD : (rr + 1) * HD] = oland[rr]
    for copy in pending:
        copy.wait_send()


def per_device(streams, short_taps, long_taps, skip_gain, norm_gain, w_qkv):
    vmem = pl.BlockSpec(memory_space=pltpu.VMEM)
    dma = pltpu.SemaphoreType.DMA
    return pl.pallas_call(
        kernel,
        out_shape=jax.ShapeDtypeStruct((TOK, 4 * HD), BF),
        in_specs=[pl.BlockSpec(memory_space=pl.ANY)] + [vmem] * 4 + [pl.BlockSpec(memory_space=pl.ANY)],
        out_specs=vmem,
        scratch_shapes=[
            pltpu.VMEM((3, TOK, CH), BF),
            pltpu.VMEM((3, 64, 4 * HD), BF),
            pltpu.VMEM((16, CH + 128), BF),
            pltpu.VMEM((16, CH + 128), BF),
            pltpu.VMEM((3, 16 + TOK, CH), F32),
            pltpu.VMEM((CH // 128, 2 * TOK + 96, 256), BF),
            pltpu.VMEM((TOK, CH), F32),
            pltpu.VMEM((TOK, CH), F32),
            pltpu.VMEM((64, 256), F32),
            pltpu.VMEM((CH // GROUP * UNIT, 256), BF),
            pltpu.VMEM((CH // GROUP * UNIT, 256), BF),
            pltpu.VMEM((2, 4, 256, CH), BF),
            pltpu.VMEM((4, 64, 3 * HD), BF),
            pltpu.VMEM((2, 2, 16, 64, 3 * HD), BF),
            pltpu.VMEM((2, 4, 256, CH), BF),
            pltpu.VMEM((2, 16, 512, HD), BF),
            pltpu.VMEM((HD, SUP), BF),
            pltpu.VMEM((HD, SUP), F32),
            pltpu.VMEM((1, SUP), F32),
            pltpu.VMEM((1, SUP), F32),
            pltpu.VMEM((2, 256, 128), F32),
            pltpu.VMEM((4, TOK, HD), BF),
            pltpu.VMEM((4, TOK, HD), BF),
            dma((2,)),
            dma((4,)), dma((4,)),
            dma((3,)), dma((3,)),
            dma((2, 2, 20)), dma((2, 2, 20)),
            dma((2, 20)), dma((2, 20)),
            dma((4, 4)), dma((4, 4)),
            dma((4, 4)), dma((4, 4)),
            dma((8, 2)), dma((8, 2)),
            dma((3,)), dma((3,)),
        ],
        compiler_params=pltpu.CompilerParams(
            collective_id=0, has_side_effects=True, vmem_limit_bytes=56 * 1024 * 1024
        ),
    )(
        streams,
        short_taps,
        long_taps,
        skip_gain.reshape(1, CH),
        norm_gain.reshape(1, 4 * CH),
        jnp.transpose(w_qkv, (1, 0, 2)),
    )


def solution(mesh):
    in_specs = (
        P(None, "ctx", "head"),
        P(None, None, "head"),
        P("head", None),
        P("head"),
        P(),
        P("ctx", None, "head"),
    )
    return jax.shard_map(
        per_device, mesh=mesh, in_specs=in_specs, out_specs=P("ctx", "head"), check_vma=False
    )
```

```python
import math

import jax
import jax.numpy as jnp
from jax import lax
from jax.experimental import pallas as pl
from jax.experimental.pallas import tpu as pltpu
from jax.sharding import PartitionSpec as P

HD = 128
TOK = 128
HALF = TOK // 2
UNIT = HALF // 2
CH = 1024
SUP = 512
SHORT = 7
GROUP = 16
MESH = pl.DeviceIdType.MESH
BF = jnp.bfloat16
F32 = jnp.float32


def kernel(
    x_hbm, st_ref, taps_ref, skip_ref, gain_ref, w_hbm, out_ref,
    x_ref, w_ref, rim_src, rim, ext, ghl, gf, x1f, base, thi, tlo, mall, wsrc, wbuf, normed, kv, qt, acc, lsum, mrow, psum, att, oland,
    l_in, s_halo, r_halo, s_w0, r_w0, s_w, r_w, s_kv, r_kv, s_zp, r_zp, s_zm, r_zm, s_oc, r_oc, s_out, r_out,
):
    c = lax.axis_index("ctx")
    zl = lax.axis_index("head")
    s = c // 4
    r = c % 4
    y, x = s // 4, s % 4
    zh, core = r // 2, r % 2
    z = zh * 4 + zl

    def dev(yy, xx, zz, cc):
        return (((yy * 4 + xx) * 2 + zz // 4) * 2 + cc, zz % 4)

    x_next, x_prev = dev(y, (x + 1) % 4, z, core), dev(y, (x + 3) % 4, z, core)
    y_next, y_prev = dev((y + 1) % 4, x, z, core), dev((y + 3) % 4, x, z, core)
    z_next, z_prev = dev(y, x, (z + 1) % 8, core), dev(y, x, (z + 7) % 8, core)
    other = dev(y, x, z, 1 - core)
    x_far, y_far = dev(y, (x + 2) % 4, z, core), dev((y + 2) % 4, x, z, core)
    mate_at = [(zh, 1 - core), (1 - zh, core), (1 - zh, 1 - core)]
    mate_rank = [a * 2 + b for a, b in mate_at]
    mates = [(s * 4 + rank, zl) for rank in mate_rank]
    c_next, c_prev = ((c + 1) % 64, zl), ((c + 63) % 64, zl)

    pending = []

    def send(src, dst, s_sem, r_sem, to):
        copy = pltpu.make_async_remote_copy(
            src_ref=src, dst_ref=dst, send_sem=s_sem, recv_sem=r_sem, device_id=to, device_id_type=MESH
        )
        copy.start()
        pending.append(copy)
        return copy

    def recv(dst, s_sem, r_sem, frm):
        pltpu.make_async_remote_copy(
            src_ref=dst, dst_ref=dst, send_sem=s_sem, recv_sem=r_sem, device_id=frm, device_id_type=MESH
        ).wait_recv()

    x_in = pltpu.make_async_copy(x_hbm, x_ref, l_in.at[0])
    x_in.start()
    w_in = pltpu.make_async_copy(w_hbm, w_ref, l_in.at[1])
    w_in.start()

    barrier = pltpu.get_barrier_semaphore()
    partners = [c_next, c_prev] + mates + [x_far, y_far, x_next, x_prev, y_next, y_prev, z_next, z_prev]
    for p in partners:
        pl.semaphore_signal(barrier, inc=1, device_id=p, device_id_type=MESH)

    def own_slot(h):
        return (1 - h) * (y * 4 + x) + h * (x * 4 + y)

    def fill(stream, _):
        ext[stream, 16:, :] = x_ref[stream].astype(F32)
        return 0

    x_in.wait()
    lax.fori_loop(0, 3, fill, 0)

    def featured(stream, lo, hi, lanes):
        total = None
        for j in range(SHORT):
            term = st_ref[stream, pl.ds(j, 1), lanes] * ext[stream, pl.ds(16 + lo - j, hi - lo), lanes]
            total = term if total is None else total + term
        return total

    def gate_rows(lo, hi):
        def slab(i, _):
            lanes = pl.ds(pl.multiple_of(i * 128, 128), 128)
            gated = featured(1, lo, hi, lanes) * featured(2, lo, hi, lanes)
            gf[lo:hi, lanes] = gated
            high = gated.astype(BF)
            ghl[i, TOK + lo : TOK + hi, :128] = high
            ghl[i, TOK + lo : TOK + hi, 128:] = (gated - high.astype(F32)).astype(BF)
            return 0
        lax.fori_loop(0, CH // 128, slab, 0)

    def x1_rows(lo, hi):
        def slab(i, _):
            lanes = pl.ds(pl.multiple_of(i * 128, 128), 128)
            x1f[lo:hi, lanes] = featured(0, lo, hi, lanes)
            return 0
        lax.fori_loop(0, CH // 128, slab, 0)

    def gated_rows(lo, count, block):
        return ghl.at[:, pl.ds(TOK * block + lo, count), pl.ds(0, 128)]

    halo = ((HALF, HALF), (16, HALF - 16), (0, 16))

    def halo_send(k):
        send(gated_rows(*halo[k], 1), gated_rows(*halo[k], 0), s_halo.at[k], r_halo.at[k], c_next)

    def halo_recv(k):
        recv(gated_rows(*halo[k], 0), s_halo.at[k], r_halo.at[k], c_prev)

    gate_rows(HALF, TOK)
    gate_rows(16, HALF)
    x1_rows(16, TOK)

    rows = jnp.concatenate([ext[i, 16 + TOK - 6 :, :] for i in range(3)], axis=0)
    rim_src[:, :CH] = rows[:16].astype(BF)
    rest = jnp.concatenate([rows[16:, i * 128 : (i + 1) * 128] for i in range(8)], axis=0)
    rim_src[:, CH:] = rest.astype(BF)

    w_in.wait()
    for rr in range(4):
        for k in range(3):
            wsrc[rr, :, k * HD : (k + 1) * HD] = w_ref[k, :, rr * HD : (rr + 1) * HD]
    wbuf[zh, core, own_slot(core)] = wsrc[r]

    pl.semaphore_wait(barrier, len(partners))
    send(rim_src, rim, s_halo.at[3], r_halo.at[3], c_next)
    halo_send(0)
    mine = wbuf.at[zh, core, own_slot(core)]

    def weights_to(k):
        send(wsrc.at[mate_rank[k]], mine, s_w0.at[k], r_w0.at[k], mates[k])

    def weights_from(k):
        zz, cc = mate_at[k]
        recv(wbuf.at[zz, cc, own_slot(cc)], s_w0.at[k], r_w0.at[k], mates[k])

    weights_to(0)
    weights_to(1)
    weights_to(2)

    def clear(i, _):
        ghl[i, :TOK, 128:] = jnp.zeros((TOK, 128), BF)
        ghl[i, 2 * TOK :, :] = jnp.zeros((96, 256), BF)
        return 0

    lax.fori_loop(0, CH // 128, clear, 0)
    halo_send(1)

    def gather_steps(buf, s_sem, r_sem, relay=False):
        mid = buf.shape[2] // 2

        def parts(h):
            first = (x, y, x_next, x_prev, y_next, y_prev, x_far)
            second = (y, x, y_next, y_prev, x_next, x_prev, y_far)
            if isinstance(h, int):
                return second if h else first
            mixed = []
            for p, q in zip(first, second):
                if isinstance(p, tuple):
                    mixed.append(tuple(i * (1 - h) + j * h for i, j in zip(p, q)))
                else:
                    mixed.append(p * (1 - h) + q * h)
            return mixed

        def slot(a, b):
            return (b % 4) * 4 + a % 4

        def whole(h, a, b):
            return buf.at[h, slot(a, b)]

        def piece(h, a, b, p):
            return buf.at[h, slot(a, b), pl.ds(p * mid, mid), :]

        def go(h, ref, idx, to):
            send(ref, ref, s_sem.at[h, idx], r_sem.at[h, idx], to)

        def come(h, ref, idx, frm):
            recv(ref, s_sem.at[h, idx], r_sem.at[h, idx], frm)

        off = (0, -1, 1, 2)

        def spread(h, i):
            a, b, fn, fp, gn, gp, ff = parts(h)
            ref = whole(h, a + off[i] + 4, b)
            go(h, ref, 4 + i, gn)
            go(h, ref, 8 + i, gp)

        def start(hs):
            for h in hs:
                a, b, fn, fp, gn, gp, ff = parts(h)
                go(h, whole(h, a, b), 0, fn)
                go(h, whole(h, a, b), 1, fp)
                if not relay:
                    go(h, whole(h, a, b), 2, ff)
            for h in hs:
                spread(h, 0)

        def near():
            for h in (0, 1):
                a, b, fn, fp, gn, gp, ff = parts(h)
                come(h, whole(h, a + 3, b), 0, fp)
                if relay:
                    go(h, piece(h, a + 3, b, 0), 2, fn)
                come(h, whole(h, a + 1, b), 1, fn)
                if relay:
                    go(h, piece(h, a + 1, b, 1), 3, fp)
            for h in (0, 1):
                spread(h, 1)
                spread(h, 2)

        def far():
            for h in (0, 1):
                a, b, fn, fp, gn, gp, ff = parts(h)
                if relay:
                    come(h, piece(h, a + 2, b, 0), 2, fp)
                    come(h, piece(h, a + 2, b, 1), 3, fn)
                else:
                    come(h, whole(h, a + 2, b), 2, ff)
                spread(h, 3)

        def across(i):
            for h in (0, 1):
                a, b, fn, fp, gn, gp, ff = parts(h)
                aa = a + off[i] + 4
                come(h, whole(h, aa, b + 3), 4 + i, gp)
                go(h, piece(h, aa, b + 3, 0), 12 + i, gn)
                come(h, whole(h, aa, b + 1), 8 + i, gn)
                go(h, piece(h, aa, b + 1, 1), 16 + i, gp)

        def last(i):
            for h in (0, 1):
                a, b, fn, fp, gn, gp, ff = parts(h)
                aa = a + off[i] + 4
                come(h, piece(h, aa, b + 2, 0), 12 + i, gp)
                come(h, piece(h, aa, b + 2, 1), 16 + i, gn)

        return start, near, far, across, last

    a_start, a_near, a_far, a_across, a_last = gather_steps(wbuf.at[zh], s_w.at[0], r_w.at[0])
    b_start, b_near, b_far, b_across, b_last = gather_steps(wbuf.at[1 - zh], s_w.at[1], r_w.at[1])

    turn = lax.broadcasted_iota(jnp.int32, (128, 256), 0) + lax.broadcasted_iota(jnp.int32, (128, 256), 1)
    turn = jnp.where(turn == 128, 1.0, 0.0).astype(BF)
    taps = taps_ref[...]
    taps_high = taps.astype(BF)
    taps_low = (taps - taps_high.astype(F32)).astype(BF)
    base[...] = jnp.dot(taps_high, turn, preferred_element_type=F32) + jnp.dot(
        taps_low, turn, preferred_element_type=F32
    )

    def build(g, _):
        row = jnp.broadcast_to(base[pl.ds(g, 1), :], (UNIT, 256))
        rows = pl.ds(pl.multiple_of(g * UNIT, UNIT), UNIT)
        rolled = pltpu.roll(row, 0, 1, stride=1, stride_axis=0)
        high = rolled.astype(BF)
        thi[rows, :] = high
        tlo[rows, :] = (rolled - high.astype(F32)).astype(BF)
        return 0

    lax.fori_loop(0, CH // GROUP, build, 0, unroll=8)

    lane_group = lax.broadcasted_iota(jnp.int32, (UNIT, 128), 1) // GROUP
    per = 128 // GROUP

    unit_at = (HALF, HALF + UNIT, UNIT, 0)

    def convolve(u):
        lo = unit_at[u]
        window = slice(lo, lo + 256)

        def slab(i, _):
            rows = pl.ds(pl.multiple_of(i * per * UNIT, per * UNIT), per * UNIT)
            both = jnp.dot(thi[rows, :], ghl[i, window, :], preferred_element_type=F32)
            rest = jnp.dot(tlo[rows, :], ghl[i, window, :128], preferred_element_type=F32)
            both = both[:, :128] + both[:, 128:] + rest
            conv = both[:UNIT]
            for g in range(1, per):
                conv = jnp.where(lane_group == g, both[g * UNIT : (g + 1) * UNIT], conv)
            lanes = pl.ds(pl.multiple_of(i * 128, 128), 128)
            mixed = x1f[lo : lo + UNIT, lanes] * (conv + skip_ref[:, lanes] * gf[lo : lo + UNIT, lanes])
            mall[zh, zl, pl.ds(pl.multiple_of(core * TOK + lo, UNIT), UNIT), lanes] = mixed.astype(BF)
            return 0

        lax.fori_loop(0, CH // 128, slab, 0, unroll=8)

    def halo_ready(k):
        halo_recv(k)
        lo, count = halo[k]

        @pl.when(first)
        def _():
            ghl[:, lo : lo + count, :128] = jnp.zeros((CH // 128, count, 128), BF)

    def rows_of(zz, cc, lo, count):
        zz = zz % 8
        return mall.at[zz // 4, zz % 4, pl.ds(cc * TOK + lo, count), :]

    def unit(zz, cc, u):
        return rows_of(zz, cc, unit_at[u], UNIT)

    def pair(zz, cc, half):
        return rows_of(zz, cc, HALF * (1 - half), HALF)

    def square(zz, cc, half):
        zz = zz % 8
        at = pl.ds(pl.multiple_of(cc * TOK + HALF * (1 - half), HALF), HALF)
        m = mall[zz // 4, zz % 4, at, :].astype(F32)
        m = m * m
        total = m[:, :128]
        for i in range(1, CH // 128):
            total = total + m[:, i * 128 : (i + 1) * 128]
        psum[zz // 4, at, :] += total

    def hand_over(zz, idx, half):
        ref = pair(zz, core, half)
        send(ref, ref, s_oc.at[idx, half], r_oc.at[idx, half], other)

    def ring_own(u):
        convolve(u)
        own = unit(z, core, u)
        send(own, own, s_zp.at[0, u], r_zp.at[0, u], z_next)
        send(own, own, s_zm.at[0, u], r_zm.at[0, u], z_prev)

    def ring_own_rest(half):
        hand_over(z, 0, half)
        square(z, core, half)

    def ring_step(k, u):
        if k < 3 or u % 2 == 0:
            ref = unit(z + 7 - k, core, u)
            recv(ref, s_zp.at[k, u], r_zp.at[k, u], z_prev)
            if k + 1 < 3 or (k + 1 == 3 and u % 2 == 0):
                send(ref, ref, s_zp.at[k + 1, u], r_zp.at[k + 1, u], z_next)
        if k < 3 or u % 2 == 1:
            ref = unit(z + 1 + k, core, u)
            recv(ref, s_zm.at[k, u], r_zm.at[k, u], z_next)
            if k + 1 < 3 or (k + 1 == 3 and u % 2 == 1):
                send(ref, ref, s_zm.at[k + 1, u], r_zm.at[k + 1, u], z_prev)

    def ring_rest(k, half):
        hand_over(z + 7 - k, 1 + k, half)
        if k < 3:
            hand_over(z + 1 + k, 5 + k, half)
        square(z + 7 - k, core, half)
        if k < 3:
            square(z + 1 + k, core, half)

    def from_other(idx, half):
        step = (0, 7, 6, 5, 4, 1, 2, 3)[idx]
        recv(pair(z + step, 1 - core, half), s_oc.at[idx, half], r_oc.at[idx, half], other)
        square(z + step, 1 - core, half)

    def weights(zz, lanes):
        pieces = []
        for i in range(4):
            for zz_hi in (0, 1):
                pieces += [wbuf[zz_hi, 0, zz * 4 + i, :, lanes], wbuf[zz_hi, 1, i * 4 + zz, :, lanes]]
        return jnp.concatenate(pieces, axis=0)

    def keys_values(zhi):
        inv = lax.rsqrt(jnp.sum(psum[zhi], axis=-1, keepdims=True) * (1.0 / (4 * CH)) + 1e-06)
        proj = None
        for zz in range(4):
            rounded = (mall[zhi, zz].astype(F32) * inv * gain_ref[:, zz * CH : (zz + 1) * CH]).astype(BF)
            normed[zhi, zz] = rounded
            part = jnp.dot(rounded, weights(zz, slice(HD, 3 * HD)), preferred_element_type=F32)
            proj = part if proj is None else proj + part
        proj = proj.astype(BF).astype(F32)
        values = jnp.transpose(proj[:, HD:]).astype(BF)
        at = own_slot(zhi)
        kv[zhi, at, :256, :] = proj[:, :HD].astype(BF)
        kv[zhi, at, 256:384, :] = values[:, :128]
        kv[zhi, at, 384:, :] = values[:, 128:]

    def queries():
        for zhi in (0, 1):
            proj = None
            for zz in range(4):
                part = jnp.dot(normed[zhi, zz], weights(zz, slice(0, HD)), preferred_element_type=F32)
                proj = part if proj is None else proj + part
            qt[:, zhi * 256 : (zhi + 1) * 256] = jnp.transpose(proj.astype(BF).astype(F32)).astype(BF)

    scale = math.log2(math.e) / math.sqrt(HD)

    def scores_of(h, index):
        return jnp.dot(kv[h, index, :256, :], qt[...], preferred_element_type=F32) * scale

    def weigh(units, probs):
        values = jnp.concatenate(
            [kv[h, index, lo : lo + 128, :] for h, index in units for lo in (256, 384)], axis=1
        )
        probs = jnp.concatenate([p.astype(BF) for p in probs], axis=0)
        return jnp.dot(values, probs, preferred_element_type=F32)

    def total_of(probs):
        total = probs[0]
        for p in probs[1:]:
            total = total + p
        return jnp.sum(total, axis=0, keepdims=True)

    def absorb_own():
        units = [(h, own_slot(h)) for h in (0, 1)]
        q_pos = lax.broadcasted_iota(jnp.int32, (256, SUP), 1)
        k_pos = lax.broadcasted_iota(jnp.int32, (256, SUP), 0)
        scores = [jnp.where(k_pos + h * 256 <= q_pos, scores_of(h, index), -1e30) for h, index in units]
        top = scores[0]
        for t in scores[1:]:
            top = jnp.maximum(top, t)
        top = jnp.max(top, axis=0, keepdims=True)
        probs = [jnp.exp2(t - top) for t in scores]
        mrow[...] = top
        lsum[...] = total_of(probs)
        acc[...] = weigh(units, probs)

    def absorb(units):
        biases = [jnp.where(block < s, 0.0, -1e30) for _, _, block in units]
        units = [unit[:2] for unit in units]
        scores = [scores_of(*unit) for unit in units]
        old = mrow[...]
        top = old
        for t, bias in zip(scores, biases):
            top = jnp.maximum(top, jnp.max(t, axis=0, keepdims=True) + bias)
        probs = [jnp.exp2(t - (top - bias)) for t, bias in zip(scores, biases)]
        alpha = jnp.exp2(old - top)
        mrow[...] = top
        lsum[...] = lsum[...] * alpha + total_of(probs)
        acc[...] = acc[...] * alpha + weigh(units, probs)

    def arrived(places):
        units = []
        for h, da, db in places:
            a, b = (x, y) if h == 0 else (y, x)
            aa, bb = (a + da + 4) % 4, (b + db + 4) % 4
            units.append((h, bb * 4 + aa, bb * 4 + aa if h == 0 else aa * 4 + bb))
        seen = units[0][2] < s
        for unit in units[1:]:
            seen = seen | (unit[2] < s)

        @pl.when(seen)
        def _():
            absorb(units)

    weights_from(0)
    a_start((0, 1))
    first = c == 0
    recv(rim, s_halo.at[3], r_halo.at[3], c_prev)
    rest = rim[:, CH:].astype(F32)
    rest = jnp.concatenate([rest[2 * i : 2 * i + 2] for i in range(8)], axis=1)
    rows = jnp.concatenate([rim[:, :CH].astype(F32), rest], axis=0)
    rows = jnp.where(first, 0.0, rows)
    for i in range(3):
        ext[i, 10:16, :] = rows[6 * i : 6 * i + 6]
    gate_rows(0, 16)
    halo_send(2)
    x1_rows(0, 16)
    psum[...] = jnp.zeros_like(psum)
    halo_ready(0)
    ring_own(0)
    ring_own(1)
    halo_ready(1)
    ring_own(2)
    ring_own_rest(0)
    a_across(0)
    a_near()
    a_far()
    weights_from(1)
    weights_from(2)
    b_start((0, 1))
    ring_step(0, 0)
    ring_step(0, 1)
    halo_ready(2)
    ring_own(3)
    ring_step(0, 2)
    ring_own_rest(1)
    ring_rest(0, 0)
    from_other(0, 0)
    a_across(1)
    a_across(2)
    a_across(3)
    ring_step(1, 0)
    ring_step(1, 1)
    ring_step(0, 3)
    ring_rest(1, 0)
    ring_rest(0, 1)
    from_other(1, 0)
    from_other(5, 0)
    ring_step(1, 2)
    b_across(0)
    b_near()
    b_far()
    from_other(0, 1)
    ring_step(2, 0)
    ring_step(2, 1)
    ring_step(1, 3)
    ring_rest(2, 0)
    ring_rest(1, 1)
    for i in range(4):
        a_last(i)
    b_across(1)
    b_across(2)
    b_across(3)
    from_other(2, 0)
    from_other(6, 0)
    from_other(1, 1)
    from_other(5, 1)
    ring_step(2, 2)
    ring_step(2, 3)
    ring_rest(2, 1)
    from_other(3, 0)
    from_other(7, 0)
    from_other(2, 1)
    from_other(6, 1)
    from_other(3, 1)
    from_other(7, 1)
    for i in range(4):
        b_last(i)
    k_start, k_near, k_far, k_across, k_last = gather_steps(kv, s_kv, r_kv, relay=True)
    keys_values(zh)
    k_start((zh,))
    ring_step(3, 0)
    ring_step(3, 1)
    ring_rest(3, 0)
    ring_step(3, 2)
    ring_step(3, 3)
    ring_rest(3, 1)
    from_other(4, 0)
    from_other(4, 1)
    keys_values(1 - zh)
    k_start((1 - zh,))
    queries()
    absorb_own()
    off = (0, -1, 1, 2)

    def across_arrived(i):
        for h in (0, 1):
            arrived([(h, off[i], -1), (h, off[i], 1)])

    k_across(0)
    k_near()
    k_far()
    across_arrived(0)
    for h in (0, 1):
        arrived([(h, -1, 0), (h, 1, 0)])
    k_across(1)
    k_across(2)
    arrived([(0, 2, 0), (1, 2, 0)])
    across_arrived(1)
    k_across(3)
    across_arrived(2)
    across_arrived(3)
    for i in range(4):
        k_last(i)
        arrived([(0, off[i], 2), (1, off[i], 2)])

    result = jnp.transpose(acc[...] / lsum[...]).astype(BF)
    for rr in range(4):
        att[rr] = result[rr * TOK : (rr + 1) * TOK]
    for k in (1, 2, 0):
        send(att.at[mate_rank[k]], oland.at[r], s_out.at[k], r_out.at[k], mates[k])
    oland[r] = att[r]
    for k in range(3):
        recv(oland.at[mate_rank[k]], s_out.at[k], r_out.at[k], mates[k])
    for rr in range(4):
        out_ref[:, rr * HD : (rr + 1) * HD] = oland[rr]
    for copy in pending:
        copy.wait_send()


def per_device(streams, short_taps, long_taps, skip_gain, norm_gain, w_qkv):
    vmem = pl.BlockSpec(memory_space=pltpu.VMEM)
    dma = pltpu.SemaphoreType.DMA
    return pl.pallas_call(
        kernel,
        out_shape=jax.ShapeDtypeStruct((TOK, 4 * HD), BF),
        in_specs=[pl.BlockSpec(memory_space=pl.ANY)] + [vmem] * 4 + [pl.BlockSpec(memory_space=pl.ANY)],
        out_specs=vmem,
        scratch_shapes=[
            pltpu.VMEM((3, TOK, CH), BF),
            pltpu.VMEM((3, 64, 4 * HD), BF),
            pltpu.VMEM((16, CH + 128), BF),
            pltpu.VMEM((16, CH + 128), BF),
            pltpu.VMEM((3, 16 + TOK, CH), F32),
            pltpu.VMEM((CH // 128, 2 * TOK + 96, 256), BF),
            pltpu.VMEM((TOK, CH), F32),
            pltpu.VMEM((TOK, CH), F32),
            pltpu.VMEM((64, 256), F32),
            pltpu.VMEM((CH // GROUP * UNIT, 256), BF),
            pltpu.VMEM((CH // GROUP * UNIT, 256), BF),
            pltpu.VMEM((2, 4, 256, CH), BF),
            pltpu.VMEM((4, 64, 3 * HD), BF),
            pltpu.VMEM((2, 2, 16, 64, 3 * HD), BF),
            pltpu.VMEM((2, 4, 256, CH), BF),
            pltpu.VMEM((2, 16, 512, HD), BF),
            pltpu.VMEM((HD, SUP), BF),
            pltpu.VMEM((HD, SUP), F32),
            pltpu.VMEM((1, SUP), F32),
            pltpu.VMEM((1, SUP), F32),
            pltpu.VMEM((2, 256, 128), F32),
            pltpu.VMEM((4, TOK, HD), BF),
            pltpu.VMEM((4, TOK, HD), BF),
            dma((2,)),
            dma((4,)), dma((4,)),
            dma((3,)), dma((3,)),
            dma((2, 2, 20)), dma((2, 2, 20)),
            dma((2, 20)), dma((2, 20)),
            dma((4, 4)), dma((4, 4)),
            dma((4, 4)), dma((4, 4)),
            dma((8, 2)), dma((8, 2)),
            dma((3,)), dma((3,)),
        ],
        compiler_params=pltpu.CompilerParams(
            collective_id=0, has_side_effects=True, vmem_limit_bytes=56 * 1024 * 1024
        ),
    )(
        streams,
        short_taps,
        long_taps,
        skip_gain.reshape(1, CH),
        norm_gain.reshape(1, 4 * CH),
        jnp.transpose(w_qkv, (1, 0, 2)),
    )


def solution(mesh):
    in_specs = (
        P(None, "ctx", "head"),
        P(None, None, "head"),
        P("head", None),
        P("head"),
        P(),
        P("ctx", None, "head"),
    )
    return jax.shard_map(
        per_device, mesh=mesh, in_specs=in_specs, out_specs=P("ctx", "head"), check_vma=False
    )
```

```python
import math

import jax
import jax.numpy as jnp
from jax import lax
from jax.experimental import pallas as pl
from jax.experimental.pallas import tpu as pltpu
from jax.sharding import PartitionSpec as P

HD = 128
TOK = 128
HALF = TOK // 2
UNIT = HALF // 2
CH = 1024
SUP = 512
SHORT = 7
GROUP = 16
MESH = pl.DeviceIdType.MESH
BF = jnp.bfloat16
F32 = jnp.float32


def kernel(
    x_hbm, st_ref, taps_ref, skip_ref, gain_ref, w_hbm, out_ref,
    x_ref, w_ref, rim_src, rim, ext, ghl, gf, x1f, base, thi, tlo, mall, wsrc, wbuf, normed, kv, qt, acc, lsum, mrow, psum, att, oland,
    l_in, s_halo, r_halo, s_w0, r_w0, s_w, r_w, s_kv, r_kv, s_zp, r_zp, s_zm, r_zm, s_oc, r_oc, s_out, r_out,
):
    c = lax.axis_index("ctx")
    zl = lax.axis_index("head")
    s = c // 4
    r = c % 4
    y, x = s // 4, s % 4
    zh, core = r // 2, r % 2
    z = zh * 4 + zl

    def dev(yy, xx, zz, cc):
        return (((yy * 4 + xx) * 2 + zz // 4) * 2 + cc, zz % 4)

    x_next, x_prev = dev(y, (x + 1) % 4, z, core), dev(y, (x + 3) % 4, z, core)
    y_next, y_prev = dev((y + 1) % 4, x, z, core), dev((y + 3) % 4, x, z, core)
    z_next, z_prev = dev(y, x, (z + 1) % 8, core), dev(y, x, (z + 7) % 8, core)
    other = dev(y, x, z, 1 - core)
    x_far, y_far = dev(y, (x + 2) % 4, z, core), dev((y + 2) % 4, x, z, core)
    mate_at = [(zh, 1 - core), (1 - zh, core), (1 - zh, 1 - core)]
    mate_rank = [a * 2 + b for a, b in mate_at]
    mates = [(s * 4 + rank, zl) for rank in mate_rank]
    c_next, c_prev = ((c + 1) % 64, zl), ((c + 63) % 64, zl)

    pending = []

    def send(src, dst, s_sem, r_sem, to):
        copy = pltpu.make_async_remote_copy(
            src_ref=src, dst_ref=dst, send_sem=s_sem, recv_sem=r_sem, device_id=to, device_id_type=MESH
        )
        copy.start()
        pending.append(copy)
        return copy

    def recv(dst, s_sem, r_sem, frm):
        pltpu.make_async_remote_copy(
            src_ref=dst, dst_ref=dst, send_sem=s_sem, recv_sem=r_sem, device_id=frm, device_id_type=MESH
        ).wait_recv()

    x_in = pltpu.make_async_copy(x_hbm, x_ref, l_in.at[0])
    x_in.start()
    w_in = pltpu.make_async_copy(w_hbm, w_ref, l_in.at[1])
    w_in.start()

    barrier = pltpu.get_barrier_semaphore()
    partners = [c_next, c_prev] + mates + [x_far, y_far, x_next, x_prev, y_next, y_prev, z_next, z_prev]
    for p in partners:
        pl.semaphore_signal(barrier, inc=1, device_id=p, device_id_type=MESH)

    def own_slot(h):
        return (1 - h) * (y * 4 + x) + h * (x * 4 + y)

    def fill(stream, _):
        ext[stream, 16:, :] = x_ref[stream].astype(F32)
        return 0

    x_in.wait()
    lax.fori_loop(0, 3, fill, 0)

    def featured(stream, lo, hi, lanes):
        total = None
        for j in range(SHORT):
            term = st_ref[stream, pl.ds(j, 1), lanes] * ext[stream, pl.ds(16 + lo - j, hi - lo), lanes]
            total = term if total is None else total + term
        return total

    def gate_rows(lo, hi):
        def slab(i, _):
            lanes = pl.ds(pl.multiple_of(i * 128, 128), 128)
            gated = featured(1, lo, hi, lanes) * featured(2, lo, hi, lanes)
            gf[lo:hi, lanes] = gated
            high = gated.astype(BF)
            ghl[i, TOK + lo : TOK + hi, :128] = high
            ghl[i, TOK + lo : TOK + hi, 128:] = (gated - high.astype(F32)).astype(BF)
            return 0
        lax.fori_loop(0, CH // 128, slab, 0)

    def x1_rows(lo, hi):
        def slab(i, _):
            lanes = pl.ds(pl.multiple_of(i * 128, 128), 128)
            x1f[lo:hi, lanes] = featured(0, lo, hi, lanes)
            return 0
        lax.fori_loop(0, CH // 128, slab, 0)

    def gated_rows(lo, count, block):
        return ghl.at[:, pl.ds(TOK * block + lo, count), pl.ds(0, 128)]

    halo = ((HALF, HALF), (16, HALF - 16), (0, 16))

    def halo_send(k):
        send(gated_rows(*halo[k], 1), gated_rows(*halo[k], 0), s_halo.at[k], r_halo.at[k], c_next)

    def halo_recv(k):
        recv(gated_rows(*halo[k], 0), s_halo.at[k], r_halo.at[k], c_prev)

    gate_rows(HALF, TOK)
    gate_rows(16, HALF)
    x1_rows(16, TOK)

    rows = jnp.concatenate([ext[i, 16 + TOK - 6 :, :] for i in range(3)], axis=0)
    rim_src[:, :CH] = rows[:16].astype(BF)
    rest = jnp.concatenate([rows[16:, i * 128 : (i + 1) * 128] for i in range(8)], axis=0)
    rim_src[:, CH:] = rest.astype(BF)

    w_in.wait()
    for rr in range(4):
        for k in range(3):
            wsrc[rr, :, k * HD : (k + 1) * HD] = w_ref[k, :, rr * HD : (rr + 1) * HD]
    wbuf[zh, core, own_slot(core)] = wsrc[r]

    pl.semaphore_wait(barrier, len(partners))
    send(rim_src, rim, s_halo.at[3], r_halo.at[3], c_next)
    halo_send(0)
    mine = wbuf.at[zh, core, own_slot(core)]

    def weights_to(k):
        send(wsrc.at[mate_rank[k]], mine, s_w0.at[k], r_w0.at[k], mates[k])

    def weights_from(k):
        zz, cc = mate_at[k]
        recv(wbuf.at[zz, cc, own_slot(cc)], s_w0.at[k], r_w0.at[k], mates[k])

    weights_to(0)
    weights_to(1)
    weights_to(2)

    def clear(i, _):
        ghl[i, :TOK, 128:] = jnp.zeros((TOK, 128), BF)
        ghl[i, 2 * TOK :, :] = jnp.zeros((96, 256), BF)
        return 0

    lax.fori_loop(0, CH // 128, clear, 0)
    halo_send(1)

    def gather_steps(buf, s_sem, r_sem, relay=False):
        mid = buf.shape[2] // 2

        def parts(h):
            first = (x, y, x_next, x_prev, y_next, y_prev, x_far)
            second = (y, x, y_next, y_prev, x_next, x_prev, y_far)
            if isinstance(h, int):
                return second if h else first
            mixed = []
            for p, q in zip(first, second):
                if isinstance(p, tuple):
                    mixed.append(tuple(i * (1 - h) + j * h for i, j in zip(p, q)))
                else:
                    mixed.append(p * (1 - h) + q * h)
            return mixed

        def slot(a, b):
            return (b % 4) * 4 + a % 4

        def whole(h, a, b):
            return buf.at[h, slot(a, b)]

        def piece(h, a, b, p):
            return buf.at[h, slot(a, b), pl.ds(p * mid, mid), :]

        def go(h, ref, idx, to):
            send(ref, ref, s_sem.at[h, idx], r_sem.at[h, idx], to)

        def come(h, ref, idx, frm):
            recv(ref, s_sem.at[h, idx], r_sem.at[h, idx], frm)

        off = (0, -1, 1, 2)

        def spread(h, i):
            a, b, fn, fp, gn, gp, ff = parts(h)
            ref = whole(h, a + off[i] + 4, b)
            go(h, ref, 4 + i, gn)
            go(h, ref, 8 + i, gp)

        def start(hs):
            for h in hs:
                a, b, fn, fp, gn, gp, ff = parts(h)
                go(h, whole(h, a, b), 0, fn)
                go(h, whole(h, a, b), 1, fp)
                if not relay:
                    go(h, whole(h, a, b), 2, ff)
            for h in hs:
                spread(h, 0)

        def near():
            for h in (0, 1):
                a, b, fn, fp, gn, gp, ff = parts(h)
                come(h, whole(h, a + 3, b), 0, fp)
                if relay:
                    go(h, piece(h, a + 3, b, 0), 2, fn)
                come(h, whole(h, a + 1, b), 1, fn)
                if relay:
                    go(h, piece(h, a + 1, b, 1), 3, fp)
            for h in (0, 1):
                spread(h, 1)
                spread(h, 2)

        def far():
            for h in (0, 1):
                a, b, fn, fp, gn, gp, ff = parts(h)
                if relay:
                    come(h, piece(h, a + 2, b, 0), 2, fp)
                    come(h, piece(h, a + 2, b, 1), 3, fn)
                else:
                    come(h, whole(h, a + 2, b), 2, ff)
                spread(h, 3)

        def across(i):
            for h in (0, 1):
                a, b, fn, fp, gn, gp, ff = parts(h)
                aa = a + off[i] + 4
                come(h, whole(h, aa, b + 3), 4 + i, gp)
                go(h, piece(h, aa, b + 3, 0), 12 + i, gn)
                come(h, whole(h, aa, b + 1), 8 + i, gn)
                go(h, piece(h, aa, b + 1, 1), 16 + i, gp)

        def last(i):
            for h in (0, 1):
                a, b, fn, fp, gn, gp, ff = parts(h)
                aa = a + off[i] + 4
                come(h, piece(h, aa, b + 2, 0), 12 + i, gp)
                come(h, piece(h, aa, b + 2, 1), 16 + i, gn)

        return start, near, far, across, last

    a_start, a_near, a_far, a_across, a_last = gather_steps(wbuf.at[zh], s_w.at[0], r_w.at[0])
    b_start, b_near, b_far, b_across, b_last = gather_steps(wbuf.at[1 - zh], s_w.at[1], r_w.at[1])

    turn = lax.broadcasted_iota(jnp.int32, (128, 256), 0) + lax.broadcasted_iota(jnp.int32, (128, 256), 1)
    turn = jnp.where(turn == 128, 1.0, 0.0).astype(BF)
    taps = taps_ref[...]
    taps_high = taps.astype(BF)
    taps_low = (taps - taps_high.astype(F32)).astype(BF)
    base[...] = jnp.dot(taps_high, turn, preferred_element_type=F32) + jnp.dot(
        taps_low, turn, preferred_element_type=F32
    )

    def build(g, _):
        row = jnp.broadcast_to(base[pl.ds(g, 1), :], (UNIT, 256))
        rows = pl.ds(pl.multiple_of(g * UNIT, UNIT), UNIT)
        rolled = pltpu.roll(row, 0, 1, stride=1, stride_axis=0)
        high = rolled.astype(BF)
        thi[rows, :] = high
        tlo[rows, :] = (rolled - high.astype(F32)).astype(BF)
        return 0

    lax.fori_loop(0, CH // GROUP, build, 0, unroll=8)

    lane_group = lax.broadcasted_iota(jnp.int32, (UNIT, 128), 1) // GROUP
    per = 128 // GROUP

    unit_at = (HALF, HALF + UNIT, UNIT, 0)

    def convolve(u):
        lo = unit_at[u]
        window = slice(lo, lo + 256)

        def slab(i, _):
            rows = pl.ds(pl.multiple_of(i * per * UNIT, per * UNIT), per * UNIT)
            both = jnp.dot(thi[rows, :], ghl[i, window, :], preferred_element_type=F32)
            rest = jnp.dot(tlo[rows, :], ghl[i, window, :128], preferred_element_type=F32)
            both = both[:, :128] + both[:, 128:] + rest
            conv = both[:UNIT]
            for g in range(1, per):
                conv = jnp.where(lane_group == g, both[g * UNIT : (g + 1) * UNIT], conv)
            lanes = pl.ds(pl.multiple_of(i * 128, 128), 128)
            mixed = x1f[lo : lo + UNIT, lanes] * (conv + skip_ref[:, lanes] * gf[lo : lo + UNIT, lanes])
            mall[zh, zl, pl.ds(pl.multiple_of(core * TOK + lo, UNIT), UNIT), lanes] = mixed.astype(BF)
            return 0

        lax.fori_loop(0, CH // 128, slab, 0, unroll=8)

    def halo_ready(k):
        halo_recv(k)
        lo, count = halo[k]

        @pl.when(first)
        def _():
            ghl[:, lo : lo + count, :128] = jnp.zeros((CH // 128, count, 128), BF)

    def rows_of(zz, cc, lo, count):
        zz = zz % 8
        return mall.at[zz // 4, zz % 4, pl.ds(cc * TOK + lo, count), :]

    def unit(zz, cc, u):
        return rows_of(zz, cc, unit_at[u], UNIT)

    def pair(zz, cc, half):
        return rows_of(zz, cc, HALF * (1 - half), HALF)

    def square(zz, cc, half):
        zz = zz % 8
        at = pl.ds(pl.multiple_of(cc * TOK + HALF * (1 - half), HALF), HALF)
        m = mall[zz // 4, zz % 4, at, :].astype(F32)
        m = m * m
        total = m[:, :128]
        for i in range(1, CH // 128):
            total = total + m[:, i * 128 : (i + 1) * 128]
        psum[zz // 4, at, :] += total

    def hand_over(zz, idx, half):
        ref = pair(zz, core, half)
        send(ref, ref, s_oc.at[idx, half], r_oc.at[idx, half], other)

    def ring_own(u):
        convolve(u)
        own = unit(z, core, u)
        send(own, own, s_zp.at[0, u], r_zp.at[0, u], z_next)
        send(own, own, s_zm.at[0, u], r_zm.at[0, u], z_prev)

    def ring_own_rest(half):
        hand_over(z, 0, half)
        square(z, core, half)

    def ring_step(k, u):
        if k < 3 or u % 2 == 0:
            ref = unit(z + 7 - k, core, u)
            recv(ref, s_zp.at[k, u], r_zp.at[k, u], z_prev)
            if k + 1 < 3 or (k + 1 == 3 and u % 2 == 0):
                send(ref, ref, s_zp.at[k + 1, u], r_zp.at[k + 1, u], z_next)
        if k < 3 or u % 2 == 1:
            ref = unit(z + 1 + k, core, u)
            recv(ref, s_zm.at[k, u], r_zm.at[k, u], z_next)
            if k + 1 < 3 or (k + 1 == 3 and u % 2 == 1):
                send(ref, ref, s_zm.at[k + 1, u], r_zm.at[k + 1, u], z_prev)

    def ring_rest(k, half):
        hand_over(z + 7 - k, 1 + k, half)
        if k < 3:
            hand_over(z + 1 + k, 5 + k, half)
        square(z + 7 - k, core, half)
        if k < 3:
            square(z + 1 + k, core, half)

    def from_other(idx, half):
        step = (0, 7, 6, 5, 4, 1, 2, 3)[idx]
        recv(pair(z + step, 1 - core, half), s_oc.at[idx, half], r_oc.at[idx, half], other)
        square(z + step, 1 - core, half)

    def weights(zz, lanes):
        pieces = []
        for i in range(4):
            for zz_hi in (0, 1):
                pieces += [wbuf[zz_hi, 0, zz * 4 + i, :, lanes], wbuf[zz_hi, 1, i * 4 + zz, :, lanes]]
        return jnp.concatenate(pieces, axis=0)

    def keys_values(zhi):
        inv = lax.rsqrt(jnp.sum(psum[zhi], axis=-1, keepdims=True) * (1.0 / (4 * CH)) + 1e-06)
        proj = None
        for zz in range(4):
            rounded = (mall[zhi, zz].astype(F32) * inv * gain_ref[:, zz * CH : (zz + 1) * CH]).astype(BF)
            normed[zhi, zz] = rounded
            part = jnp.dot(rounded, weights(zz, slice(HD, 3 * HD)), preferred_element_type=F32)
            proj = part if proj is None else proj + part
        proj = proj.astype(BF).astype(F32)
        values = jnp.transpose(proj[:, HD:]).astype(BF)
        at = own_slot(zhi)
        kv[zhi, at, :256, :] = proj[:, :HD].astype(BF)
        kv[zhi, at, 256:384, :] = values[:, :128]
        kv[zhi, at, 384:, :] = values[:, 128:]

    def queries():
        for zhi in (0, 1):
            proj = None
            for zz in range(4):
                part = jnp.dot(normed[zhi, zz], weights(zz, slice(0, HD)), preferred_element_type=F32)
                proj = part if proj is None else proj + part
            qt[:, zhi * 256 : (zhi + 1) * 256] = jnp.transpose(proj.astype(BF).astype(F32)).astype(BF)

    scale = math.log2(math.e) / math.sqrt(HD)

    def scores_of(h, index):
        return jnp.dot(kv[h, index, :256, :], qt[...], preferred_element_type=F32) * scale

    def weigh(units, probs):
        values = jnp.concatenate(
            [kv[h, index, lo : lo + 128, :] for h, index in units for lo in (256, 384)], axis=1
        )
        probs = jnp.concatenate([p.astype(BF) for p in probs], axis=0)
        return jnp.dot(values, probs, preferred_element_type=F32)

    def total_of(probs):
        total = probs[0]
        for p in probs[1:]:
            total = total + p
        return jnp.sum(total, axis=0, keepdims=True)

    def absorb_own():
        units = [(h, own_slot(h)) for h in (0, 1)]
        q_pos = lax.broadcasted_iota(jnp.int32, (256, SUP), 1)
        k_pos = lax.broadcasted_iota(jnp.int32, (256, SUP), 0)
        scores = [jnp.where(k_pos + h * 256 <= q_pos, scores_of(h, index), -1e30) for h, index in units]
        top = scores[0]
        for t in scores[1:]:
            top = jnp.maximum(top, t)
        top = jnp.max(top, axis=0, keepdims=True)
        probs = [jnp.exp2(t - top) for t in scores]
        mrow[...] = top
        lsum[...] = total_of(probs)
        acc[...] = weigh(units, probs)

    def absorb(units):
        biases = [jnp.where(block < s, 0.0, -1e30) for _, _, block in units]
        units = [unit[:2] for unit in units]
        scores = [scores_of(*unit) for unit in units]
        old = mrow[...]
        top = old
        for t, bias in zip(scores, biases):
            top = jnp.maximum(top, jnp.max(t, axis=0, keepdims=True) + bias)
        probs = [jnp.exp2(t - (top - bias)) for t, bias in zip(scores, biases)]
        alpha = jnp.exp2(old - top)
        mrow[...] = top
        lsum[...] = lsum[...] * alpha + total_of(probs)
        acc[...] = acc[...] * alpha + weigh(units, probs)

    def arrived(places):
        units = []
        for h, da, db in places:
            a, b = (x, y) if h == 0 else (y, x)
            aa, bb = (a + da + 4) % 4, (b + db + 4) % 4
            units.append((h, bb * 4 + aa, bb * 4 + aa if h == 0 else aa * 4 + bb))
        seen = units[0][2] < s
        for unit in units[1:]:
            seen = seen | (unit[2] < s)

        @pl.when(seen)
        def _():
            absorb(units)

    weights_from(0)
    a_start((0, 1))
    first = c == 0
    recv(rim, s_halo.at[3], r_halo.at[3], c_prev)
    rest = rim[:, CH:].astype(F32)
    rest = jnp.concatenate([rest[2 * i : 2 * i + 2] for i in range(8)], axis=1)
    rows = jnp.concatenate([rim[:, :CH].astype(F32), rest], axis=0)
    rows = jnp.where(first, 0.0, rows)
    for i in range(3):
        ext[i, 10:16, :] = rows[6 * i : 6 * i + 6]
    gate_rows(0, 16)
    halo_send(2)
    x1_rows(0, 16)
    psum[...] = jnp.zeros_like(psum)
    halo_ready(0)
    ring_own(0)
    ring_own(1)
    halo_ready(1)
    ring_own(2)
    ring_own_rest(0)
    weights_from(1)
    weights_from(2)
    b_start((0, 1))
    a_across(0)
    a_near()
    a_far()
    ring_step(0, 0)
    ring_step(0, 1)
    halo_ready(2)
    ring_own(3)
    ring_step(0, 2)
    ring_own_rest(1)
    ring_rest(0, 0)
    from_other(0, 0)
    a_across(1)
    a_across(2)
    a_across(3)
    ring_step(1, 0)
    ring_step(1, 1)
    ring_step(0, 3)
    ring_rest(1, 0)
    ring_rest(0, 1)
    from_other(1, 0)
    from_other(5, 0)
    ring_step(1, 2)
    b_across(0)
    b_near()
    b_far()
    from_other(0, 1)
    ring_step(2, 0)
    ring_step(2, 1)
    ring_step(1, 3)
    ring_rest(2, 0)
    ring_rest(1, 1)
    for i in range(4):
        a_last(i)
    b_across(1)
    b_across(2)
    b_across(3)
    from_other(2, 0)
    from_other(6, 0)
    from_other(1, 1)
    from_other(5, 1)
    ring_step(2, 2)
    ring_step(2, 3)
    ring_rest(2, 1)
    from_other(3, 0)
    from_other(7, 0)
    from_other(2, 1)
    from_other(6, 1)
    from_other(3, 1)
    from_other(7, 1)
    for i in range(4):
        b_last(i)
    k_start, k_near, k_far, k_across, k_last = gather_steps(kv, s_kv, r_kv, relay=True)
    keys_values(zh)
    k_start((zh,))
    ring_step(3, 0)
    ring_step(3, 1)
    ring_rest(3, 0)
    ring_step(3, 2)
    ring_step(3, 3)
    ring_rest(3, 1)
    from_other(4, 0)
    from_other(4, 1)
    keys_values(1 - zh)
    k_start((1 - zh,))
    queries()
    absorb_own()
    off = (0, -1, 1, 2)

    def across_arrived(i):
        for h in (0, 1):
            arrived([(h, off[i], -1), (h, off[i], 1)])

    k_across(0)
    k_near()
    k_far()
    across_arrived(0)
    for h in (0, 1):
        arrived([(h, -1, 0), (h, 1, 0)])
    k_across(1)
    k_across(2)
    arrived([(0, 2, 0), (1, 2, 0)])
    across_arrived(1)
    k_across(3)
    across_arrived(2)
    across_arrived(3)
    for i in range(4):
        k_last(i)
        arrived([(0, off[i], 2), (1, off[i], 2)])

    result = jnp.transpose(acc[...] / lsum[...]).astype(BF)
    for rr in range(4):
        att[rr] = result[rr * TOK : (rr + 1) * TOK]
    for k in (1, 2, 0):
        send(att.at[mate_rank[k]], oland.at[r], s_out.at[k], r_out.at[k], mates[k])
    oland[r] = att[r]
    for k in range(3):
        recv(oland.at[mate_rank[k]], s_out.at[k], r_out.at[k], mates[k])
    for rr in range(4):
        out_ref[:, rr * HD : (rr + 1) * HD] = oland[rr]
    for copy in pending:
        copy.wait_send()


def per_device(streams, short_taps, long_taps, skip_gain, norm_gain, w_qkv):
    vmem = pl.BlockSpec(memory_space=pltpu.VMEM)
    dma = pltpu.SemaphoreType.DMA
    return pl.pallas_call(
        kernel,
        out_shape=jax.ShapeDtypeStruct((TOK, 4 * HD), BF),
        in_specs=[pl.BlockSpec(memory_space=pl.ANY)] + [vmem] * 4 + [pl.BlockSpec(memory_space=pl.ANY)],
        out_specs=vmem,
        scratch_shapes=[
            pltpu.VMEM((3, TOK, CH), BF),
            pltpu.VMEM((3, 64, 4 * HD), BF),
            pltpu.VMEM((16, CH + 128), BF),
            pltpu.VMEM((16, CH + 128), BF),
            pltpu.VMEM((3, 16 + TOK, CH), F32),
            pltpu.VMEM((CH // 128, 2 * TOK + 96, 256), BF),
            pltpu.VMEM((TOK, CH), F32),
            pltpu.VMEM((TOK, CH), F32),
            pltpu.VMEM((64, 256), F32),
            pltpu.VMEM((CH // GROUP * UNIT, 256), BF),
            pltpu.VMEM((CH // GROUP * UNIT, 256), BF),
            pltpu.VMEM((2, 4, 256, CH), BF),
            pltpu.VMEM((4, 64, 3 * HD), BF),
            pltpu.VMEM((2, 2, 16, 64, 3 * HD), BF),
            pltpu.VMEM((2, 4, 256, CH), BF),
            pltpu.VMEM((2, 16, 512, HD), BF),
            pltpu.VMEM((HD, SUP), BF),
            pltpu.VMEM((HD, SUP), F32),
            pltpu.VMEM((1, SUP), F32),
            pltpu.VMEM((1, SUP), F32),
            pltpu.VMEM((2, 256, 128), F32),
            pltpu.VMEM((4, TOK, HD), BF),
            pltpu.VMEM((4, TOK, HD), BF),
            dma((2,)),
            dma((4,)), dma((4,)),
            dma((3,)), dma((3,)),
            dma((2, 2, 20)), dma((2, 2, 20)),
            dma((2, 20)), dma((2, 20)),
            dma((4, 4)), dma((4, 4)),
            dma((4, 4)), dma((4, 4)),
            dma((8, 2)), dma((8, 2)),
            dma((3,)), dma((3,)),
        ],
        compiler_params=pltpu.CompilerParams(
            collective_id=0, has_side_effects=True, vmem_limit_bytes=56 * 1024 * 1024
        ),
    )(
        streams,
        short_taps,
        long_taps,
        skip_gain.reshape(1, CH),
        norm_gain.reshape(1, 4 * CH),
        jnp.transpose(w_qkv, (1, 0, 2)),
    )


def solution(mesh):
    in_specs = (
        P(None, "ctx", "head"),
        P(None, None, "head"),
        P("head", None),
        P("head"),
        P(),
        P("ctx", None, "head"),
    )
    return jax.shard_map(
        per_device, mesh=mesh, in_specs=in_specs, out_specs=P("ctx", "head"), check_vma=False
    )
```
